32 devices in a mesh: tile: 8 (over y, x, core), fsdp: 4 (over z).
Axes of the slice: x: 2, y: 2, z: 4, core: 2. Of those that a mesh axis runs over, the one named last changes fastest.
Arguments:
- images: bfloat16 [4, 8, 8, 128, 320], P('fsdp', 'tile'), may hold values from -80 to 80
- tile_rows: int32 [4, 8], P('fsdp', 'tile'), may hold values from 1 to 8, 40 in all within a row
- cotangent: bfloat16 [4, 8, 8, 128, 320], P('fsdp', 'tile'), may hold values from -6 to 6
- master_weight: float32 [2880, 320], P('fsdp'), may hold values from -0.109375 to 0.109375
- norm_gain: float32 [320], replicated, may hold values from 0.5 to 1.5
- norm_bias: float32 [320], replicated, may hold values from -3 to 3
- first_moment: float32 [2880, 320], P('fsdp'), may hold values from -6 to 6
- second_moment: float32 [2880, 320], P('fsdp'), may hold values from 0.5 to 4
Outputs:
- activation: bfloat16 [4, 8, 8, 128, 320], P('fsdp', 'tile')
- image_grad: bfloat16 [4, 8, 8, 128, 320], P('fsdp', 'tile')
- weight_grad: float32 [2880, 320], P('fsdp')
- new_weight: float32 [2880, 320], P('fsdp')
- new_first: float32 [2880, 320], P('fsdp')
- new_second: float32 [2880, 320], P('fsdp')
- gain_grad: float32 [320], replicated
- bias_grad: float32 [320], replicated
The draws below stay inside these ranges and needn't reach their ends.
Inputs may be any that keep to these rules, and one draw needn't show every extreme that they name: `tile_rows`: in each frame the 8 counts sum to 40 and the largest is exactly 8.
All inputs are finite; a program needn't handle non-finite values. No bound on the sum of `tile_rows` on one device may be relied on, other than what follows from the above.
Results may differ from the reference program's by a relative error of at most 0.027.
Values may be sent and summed in bfloat16 or wider, within the bound.
A program may use at most 64 MiB of HBM per device.

```python
import math
import jax
import jax.numpy as jnp
import numpy as np
from jax import lax

C = 320
GROUPS = 32
COLS = 128
CAP = 8
FRAMES = 4
FRAME_ROWS = 40
CELLS = 20480
N_TILE = 8


def draw_images(key, part):
    k_base, k_chan, k_row, k_mean = jax.random.split(key, 4)
    shape = (FRAMES, N_TILE, CAP, COLS, C)
    common = 0.5 * jnp.clip(jax.random.normal(k_mean, (FRAMES, 1, 1, 1, C), jnp.float32), -2.0, 2.0)
    base = jnp.clip(jax.random.normal(k_base, shape, jnp.float32), -3.0, 3.0) + common
    position = jnp.arange(N_TILE, dtype=jnp.float32) / max(N_TILE - 1, 1)
    along = jnp.exp(position * math.log(3.0)).reshape(1, N_TILE, 1, 1, 1)
    channel_scale = jnp.exp(jax.random.uniform(k_chan, (FRAMES, 1, 1, 1, C), jnp.float32) * math.log(10.0)) / 3.0
    row_scale = jnp.exp(jax.random.uniform(k_row, (FRAMES, N_TILE, CAP, 1, 1), jnp.float32) * math.log(2.0))
    return (base * along * channel_scale * row_scale).astype(jnp.bfloat16)


def block_levels(own_key, shape, cuts, least, high):
    gain, own = 1.0, jax.random.fold_in(own_key, 6)
    for dim, shards_of in cuts:
        draws = jnp.exp(jax.random.uniform(jax.random.fold_in(own, dim), (shards_of,), jnp.float32, least / len(cuts), high / len(cuts)))
        gain = gain * jnp.repeat(draws, shape[dim] // shards_of).reshape([-1 if axis == dim else 1 for axis in range(len(shape))])
    return gain


def length_profile(amount, total, reach, skew):
    loads = [(1 << 20) // math.isqrt(standing ** skew) + 1 for standing in range(2, amount + 1)]
    surplus, given = total - reach - (amount - 1), [1] * (amount - 1)
    while surplus > 0:
        free = [i for i in range(amount - 1) if given[i] < reach]
        whole, budget = sum([loads[i] for i in free]), surplus
        for i in free:
            addition = min(reach - given[i], max(1, budget * loads[i] // whole), surplus)
            given[i] = given[i] + addition
            surplus = surplus - addition
    return np.array([reach] + given)


def uneven_parts(key, amount, total, most, lean):
    if amount == 2:
        one = jax.random.randint(key, (), max(1, total - most), min(most, total - 1) + 1)
        return jnp.stack([one, total - one])
    tallies = jnp.asarray(length_profile(amount, total, most, lean), jnp.int32)
    couples = (amount - 1) // 2
    giver, sink = tallies[1:1 + 2 * couples:2], tallies[2:2 + 2 * couples:2]
    slack = jnp.minimum(giver - 1, most - sink)
    passed = jax.random.randint(jax.random.fold_in(key, 1), (couples,), 0, 1 << 20) % (slack + 1)
    tallies = tallies.at[1:1 + 2 * couples:2].set(giver - passed).at[2:2 + 2 * couples:2].set(sink + passed)
    return tallies[jax.random.permutation(jax.random.fold_in(key, 2), amount)]


def bell_draw(own_key, dims, deviation, reach, cuts=(), kind=jnp.bfloat16):
    gain = block_levels(own_key, dims, cuts, -0.22, 0.18) if cuts else 1.0
    array = jax.random.normal(own_key, dims, jnp.float32) * deviation * gain
    return jnp.minimum(jnp.maximum(array, -reach), reach).astype(kind)


def setup_inputs(seed: int = 0) -> dict:
    keys = jax.random.split(jax.random.key(seed), 9)
    return {
        "images": draw_images(jax.random.fold_in(keys[8], 71), 0),
        "tile_rows": jax.vmap(lambda own: uneven_parts(own, N_TILE, FRAME_ROWS, CAP, 2))(jax.random.split(keys[1], FRAMES)).reshape((FRAMES, N_TILE)).astype(jnp.int32),
        "cotangent": bell_draw(keys[2], (FRAMES, N_TILE, CAP, COLS, C), 1.0, 6.0, ((0, 4), (1, 8))),
        "master_weight": bell_draw(keys[3], (9 * C, C), (9 * C) ** -0.5, 0.109375, ((0, 4),), jnp.float32),
        "norm_gain": jnp.clip(1.0 + 0.1 * jax.random.normal(keys[4], (C,), jnp.float32), 0.5, 1.5),
        "norm_bias": bell_draw(keys[5], (C,), 0.5, 3.0, (), jnp.float32),
        "first_moment": bell_draw(keys[6], (9 * C, C), 1.0, 6.0, ((0, 4),), jnp.float32),
        "second_moment": jnp.clip(jnp.exp(math.log(4.0) - 2.0794415 * jax.random.uniform(keys[7], (9 * C, C), jnp.float32) ** block_levels(keys[7], (9 * C, C), ((0, 4),), -0.2, 0.2)), 0.5, 4.0),
    }


def shifted_taps(picture):
    height, breadth = (picture.shape[0], picture.shape[1])
    padded = jnp.pad(picture, ((1, 1), (1, 1), (0, 0)))
    return [padded[row_step:row_step + height, col_step:col_step + breadth, :] for row_step in range(3) for col_step in range(3)]

def convolve(picture, kernel):
    channels = picture.shape[2]
    output = jnp.zeros((picture.shape[0] * picture.shape[1], kernel.shape[1]), jnp.float32)
    for tap_index, piece in enumerate(shifted_taps(picture)):
        output = output + jnp.dot(piece.reshape(-1, channels), kernel[tap_index * channels:(tap_index + 1) * channels], preferred_element_type=jnp.float32)
    return output

def reference(images, tile_rows, cotangent, master_weight, norm_gain, norm_bias, first_moment, second_moment):
    per_group = C // GROUPS
    kernel = master_weight.astype(jnp.bfloat16)
    flipped = kernel.reshape(9, C, C)[::-1].transpose(0, 2, 1).reshape(9 * C, C)
    population = jnp.float32(FRAME_ROWS * COLS * per_group)

    def grouped(values):
        return lax.optimization_barrier(jnp.sum(values.reshape(-1, GROUPS, per_group), axis=(0, 2)))

    def spread(stat):
        return jnp.repeat(stat, per_group)

    def one_frame(carry, inputs):
        kernel_sum, gain_sum, bias_sum = carry
        pictures, counts, upstream_in = inputs
        offsets = (jnp.cumsum(counts) - counts).astype(jnp.int32)
        slot_index = jnp.arange(CAP, dtype=jnp.int32)
        live = slot_index[None, :] < counts[:, None]
        target = jnp.where(live, offsets[:, None] + slot_index[None, :], FRAME_ROWS).reshape(-1).astype(jnp.int32)

        def compact(slot_data):
            holder = jnp.zeros((FRAME_ROWS + 1, COLS, C), slot_data.dtype)
            return holder.at[target].set(slot_data.reshape(-1, COLS, C))[:FRAME_ROWS]

        def expand(frame_data):
            extended = jnp.concatenate([frame_data, jnp.zeros((1, COLS, C), frame_data.dtype)], axis=0)
            return extended[target].reshape(N_TILE, CAP, COLS, C)
        picture = compact(pictures)
        mixed = convolve(picture, kernel)
        group_mean = grouped(mixed) / population
        centered = mixed - spread(group_mean)
        variance = grouped(centered * centered) / population
        inverse = lax.rsqrt(variance + 1e-05)
        normed = centered * spread(inverse)
        shifted = normed * norm_gain + norm_bias
        gate_value = jax.nn.sigmoid(shifted)
        activation = (shifted * gate_value).astype(jnp.bfloat16)
        upstream = compact(upstream_in).reshape(-1, C).astype(jnp.float32)
        dshift = upstream * gate_value * (1.0 + shifted * (1.0 - gate_value))
        scaled = dshift * norm_gain
        delta_mean = grouped(scaled) / population
        cross_mean = grouped(scaled * normed) / population
        pre_grad = (spread(inverse) * (scaled - spread(delta_mean) - normed * spread(cross_mean))).astype(jnp.bfloat16)
        grad_picture = pre_grad.reshape(FRAME_ROWS, COLS, C)
        image_grad = convolve(grad_picture, flipped).astype(jnp.bfloat16)
        blocks = [jnp.dot(piece.reshape(-1, C).T, pre_grad, preferred_element_type=jnp.float32) for piece in shifted_taps(picture)]
        kernel_sum = kernel_sum + jnp.concatenate(blocks, axis=0)
        gain_sum = gain_sum + lax.optimization_barrier(jnp.sum(dshift * normed, axis=0))
        bias_sum = bias_sum + lax.optimization_barrier(jnp.sum(dshift, axis=0))
        outputs = (expand(activation.reshape(FRAME_ROWS, COLS, C)), expand(image_grad.reshape(FRAME_ROWS, COLS, C)))
        return ((kernel_sum, gain_sum, bias_sum), outputs)
    start_carry = (jnp.zeros((9 * C, C), jnp.float32), jnp.zeros((C,), jnp.float32), jnp.zeros((C,), jnp.float32))
    totals, stacked = lax.scan(one_frame, start_carry, (images, tile_rows, cotangent))
    norm_scale = jnp.float32(CELLS) ** (-0.5)
    weight_grad = totals[0] * norm_scale
    new_first = 0.9 * first_moment + 0.1 * weight_grad
    new_second = 0.999 * second_moment + 0.001 * weight_grad * weight_grad
    first_fix = new_first / (1.0 - 0.9 ** 10)
    second_fix = new_second / (1.0 - 0.999 ** 10)
    new_weight = master_weight - 0.01 * first_fix / (jnp.sqrt(second_fix) + 1e-08)
    return (stacked[0], stacked[1], weight_grad, new_weight, new_first, new_second, totals[1] * norm_scale, totals[2] * norm_scale)
```

```python
import functools

import jax
import jax.numpy as jnp
from jax import lax
from jax.experimental import pallas as pl
from jax.experimental.pallas import tpu as pltpu
from jax.sharding import PartitionSpec as P

GROUPS = 32
ROWS_MEAN = 5
MESH = pl.DeviceIdType.MESH
F32 = jnp.float32
BF16 = jnp.bfloat16


def row_pieces(total, shards, shard, part, block):
    found = []
    for f in range(shards):
        for p in range(-(-shard // part)):
            low, high = f * shard + p * part, f * shard + min(shard, (p + 1) * part)
            at = low
            while at < high:
                end = min(high, (at // block + 1) * block)
                found.append((f, p, at - low, end - at, at // block, at % block))
                at = end
    return found


def kernel(
    tiles, shards, part,
    rows_ref, x_ref, ct_ref, w_ref, gain_ref, bias_ref, m1_ref, m2_ref, same_ref,
    act_ref, ig_ref, wg_ref, nw_ref, n1_ref, n2_ref, gg_ref, bg_ref,
    gath, wb, wt, wide, xcat, xcat_t, cat, y0, y1, y2, up, g0, g1, g2,
    hs, hr, hs2, hr2, st, sd, sz,
    dwbuf, dwf, sbuf, pbuf, qbuf, zbuf, rbuf, fbuf,
    z_s, z_r, p_s, p_r, s_s, s_r, h_s, h_r, h2_s, h2_r, st_s, st_r, sd_s, sd_r, sz_s, sz_r,
    b_s, b_r, q_s, q_r, r_s, r_r, f_s, f_r, e_s, e_r,
):
    slots, cols, chan = x_ref.shape
    cells = slots * cols
    shard = w_ref.shape[0]
    total = shards * shard
    chips = tiles // 2
    t = lax.axis_index("tile")
    f = lax.axis_index("fsdp")
    ch, c = t // 2, t % 2
    sibling = ch * 2 + (1 - c)
    live = rows_ref[0, 0]
    aligned = shard % 16 == 0
    sent = []

    def peer_chip(j):
        return lax.rem(ch + j, chips)

    def from_chip(j):
        return lax.rem(ch + chips - j, chips)

    def copy(src, dst, send, recv, to_tile, to_shard):
        return pltpu.make_async_remote_copy(
            src_ref=src, dst_ref=dst, send_sem=send, recv_sem=recv,
            device_id=(to_tile, to_shard), device_id_type=MESH,
        )

    def push(*args):
        made = copy(*args)
        made.start()
        sent.append(made)

    barrier = pltpu.get_barrier_semaphore()
    for j in range(1, tiles):
        pl.semaphore_signal(barrier, inc=1, device_id=(lax.rem(t + j, tiles), f), device_id_type=MESH)
    for k in range(1, shards):
        pl.semaphore_signal(barrier, inc=1, device_id=(t, lax.rem(f + k, shards)), device_id_type=MESH)

    for p in range(tiles):
        low, high = p * part, min(shard, (p + 1) * part)
        if high <= low:
            gath[f, p] = jnp.zeros((part, chan), BF16)
        else:
            rows = w_ref[low:high, :]
            if high - low < part:
                rows = jnp.concatenate([rows, jnp.zeros((part - high + low, chan), F32)], axis=0)
            gath[f, p] = rows.astype(BF16)
    hs[0] = x_ref[0]
    hs[1] = x_ref[jnp.clip(live - 1, 0, slots - 1)]
    pl.semaphore_wait(barrier, tiles + shards - 2)

    for k in range(1, shards):
        push(gath.at[f, t], gath.at[f, t], z_s.at[k - 1], z_r.at[k - 1], t, lax.rem(f + k, shards))

    def halo_copies(src, dst, send, recv):
        up_copy = copy(src.at[0], dst.at[1], send.at[0], recv.at[1], lax.rem(t + tiles - 1, tiles), f)
        down_copy = copy(src.at[1], dst.at[0], send.at[1], recv.at[0], lax.rem(t + 1, tiles), f)
        return up_copy, down_copy

    def halo_start(src, dst, send, recv):
        up_copy, down_copy = halo_copies(src, dst, send, recv)

        @pl.when(t > 0)
        def _():
            up_copy.start()

        @pl.when(t == 0)
        def _():
            dst[0] = jnp.zeros((cols, chan), BF16)

        @pl.when(t < tiles - 1)
        def _():
            down_copy.start()

        @pl.when(t == tiles - 1)
        def _():
            dst[1] = jnp.zeros((cols, chan), BF16)

    def halo_wait(src, dst, send, recv):
        up_copy, down_copy = halo_copies(src, dst, send, recv)

        @pl.when(t > 0)
        def _():
            up_copy.wait_send()
            down_copy.wait_recv()

        @pl.when(t < tiles - 1)
        def _():
            down_copy.wait_send()
            up_copy.wait_recv()

    halo_start(hs, hr, h_s, h_r)

    for k in range(1, shards):
        fs = lax.rem(f + shards - k, shards)
        block = gath.at[fs, t]
        copy(block, block, z_s.at[k - 1], z_r.at[k - 1], t, f).wait_recv()
        for j in range(1, chips):
            push(block, block, p_s.at[k - 1, j - 1], p_r.at[k - 1, j - 1], peer_chip(j) * 2 + c, f)
        push(block, block, s_s.at[k - 1, 0], s_r.at[k - 1, 0], sibling, f)

    halo_wait(hs, hr, h_s, h_r)
    below = hr[1].astype(F32)

    def is_live(r):
        return (r < live).astype(F32)

    def is_end(r):
        return (r == live).astype(F32)

    for j in range(slots + 2):
        if j == 0:
            value = hr[0].astype(F32)
        elif j <= slots:
            value = x_ref[j - 1].astype(F32) * is_live(j - 1) + below * is_end(j - 1)
        else:
            value = below * is_end(slots)
        flat, turned = value.astype(BF16), value.T.astype(BF16)
        for a in range(3):
            r = j - a
            if 0 <= r < slots:
                xcat[r * cols:(r + 1) * cols, a * chan:(a + 1) * chan] = flat
                xcat_t[a * chan:(a + 1) * chan, r * cols:(r + 1) * cols] = turned

    for k in range(1, shards):
        fs = lax.rem(f + shards - k, shards)
        for j in range(1, chips):
            block = gath.at[fs, from_chip(j) * 2 + c]
            copy(block, block, p_s.at[k - 1, j - 1], p_r.at[k - 1, j - 1], t, f).wait_recv()
            push(block, block, s_s.at[k - 1, j], s_r.at[k - 1, j], sibling, f)
    for k in range(1, shards):
        fs = lax.rem(f + shards - k, shards)
        for j in range(chips):
            block = gath.at[fs, from_chip(j) * 2 + (1 - c)]
            copy(block, block, s_s.at[k - 1, j], s_r.at[k - 1, j], sibling, f).wait_recv()

    pieces = row_pieces(total, shards, shard, part, chan)
    if aligned:
        for fi, p, low, size, tap, at in pieces:
            a, b = tap // 3, tap % 3
            wb[b, a * chan + at:a * chan + at + size, :] = gath[fi, p, low:low + size, :]
    else:
        for fi in range(shards):
            for p in range(-(-shard // part)):
                size = min(shard - p * part, part)
                dwf[fi * shard + p * part:fi * shard + p * part + size, :] = (
                    gath[fi, p].astype(F32)[:size]
                )
        for tap in range(9):
            a, b = tap // 3, tap % 3
            wb[b, a * chan:(a + 1) * chan, :] = dwf[tap * chan:(tap + 1) * chan, :].astype(BF16)

    half = cells // 2

    def three(source, weights, order):
        @pl.loop(0, 2)
        def _(h):
            at = pl.ds(pl.multiple_of(h * half, half), half)
            left = source[at, :]
            for b, into in zip(order, (y0, y1, y2)):
                into[at, :] = jnp.dot(left, weights[b], preferred_element_type=F32)

    column = lax.broadcasted_iota(jnp.int32, (cols, chan), 0)

    def later(rows):
        return jnp.where(column == 0, 0.0, pltpu.roll(rows, 1, 0))

    def earlier(rows):
        return jnp.where(column == cols - 1, 0.0, pltpu.roll(rows, cols - 1, 0))

    def span(r):
        return pl.ds(pl.multiple_of(r * cols, cols), cols)

    def group_sum(row):
        return jnp.dot(row, same_ref[...], precision=lax.Precision.HIGHEST, preferred_element_type=F32)

    three(xcat, wb, (0, 1, 2))

    def mix(r, sums):
        rows = y1[span(r), :] + later(y0[span(r), :]) + earlier(y2[span(r), :])
        y1[span(r), :] = rows
        return sums + jnp.sum(rows, axis=0, keepdims=True) * is_live(r)

    zero_row = jnp.zeros((1, chan), F32)
    own_count = live.astype(F32) * (cols * (chan // GROUPS))
    count_row = jnp.zeros((1, chan), F32) + own_count
    own_mean = group_sum(lax.fori_loop(0, slots, mix, zero_row)) / count_row

    def squares(r, sums):
        off = y1[span(r), :] - own_mean
        return sums + jnp.sum(off * off, axis=0, keepdims=True) * is_live(r)

    own_square = group_sum(lax.fori_loop(0, slots, squares, zero_row))

    def tile_share(buffer, send, recv):
        for j in range(1, tiles):
            push(buffer.at[t], buffer.at[t], send.at[j - 1], recv.at[j - 1], lax.rem(t + j, tiles), f)

    def tile_wait(buffer, send, recv):
        for j in range(1, tiles):
            block = buffer.at[lax.rem(t + tiles - j, tiles)]
            copy(block, block, send.at[j - 1], recv.at[j - 1], t, f).wait_recv()

    st[t] = jnp.concatenate(
        [own_mean, own_square, count_row, jnp.zeros((5, chan), F32)], axis=0
    )
    tile_share(st, st_s, st_r)

    for tap in range(9):
        a, b = tap // 3, tap % 3
        block = wb[b, a * chan:(a + 1) * chan, :].astype(F32)
        wt[b, a * chan:(a + 1) * chan, :] = block.T.astype(BF16)

    tile_wait(st, st_s, st_r)
    population = float(ROWS_MEAN * tiles * cols * (chan // GROUPS))
    mean = zero_row
    for i in range(tiles):
        mean = mean + st[i, 0:1, :] * st[i, 2:3, :]
    mean = mean / population
    spread = zero_row
    for i in range(tiles):
        apart = st[i, 0:1, :] - mean
        spread = spread + st[i, 1:2, :] + st[i, 2:3, :] * apart * apart
    inverse = lax.rsqrt(spread / population + 1e-05)
    gain, bias = gain_ref[...], bias_ref[...]

    def gate(r, sums):
        gains, biases = sums
        mask = is_live(r)
        normed = (y1[span(r), :] - mean) * inverse
        shifted = normed * gain + bias
        s = jax.nn.sigmoid(shifted)
        act_ref[r] = (shifted * s * mask).astype(BF16)
        dshift = ct_ref[r].astype(F32) * mask * s * (1.0 + shifted * (1.0 - s))
        y1[span(r), :] = normed
        up[span(r), :] = dshift
        return (
            gains + jnp.sum(dshift * normed, axis=0, keepdims=True),
            biases + jnp.sum(dshift, axis=0, keepdims=True),
        )

    own_gain, own_bias = lax.fori_loop(0, slots, gate, (zero_row, zero_row))
    sd[t] = jnp.concatenate([own_gain, own_bias, jnp.zeros((6, chan), F32)], axis=0)
    tile_share(sd, sd_s, sd_r)
    tile_wait(sd, sd_s, sd_r)
    frame = sd[0]
    for i in range(1, tiles):
        frame = frame + sd[i]
    sz[f] = frame
    for k in range(1, shards):
        push(sz.at[f], sz.at[f], sz_s.at[k - 1], sz_r.at[k - 1], t, lax.rem(f + k, shards))
    delta = group_sum(frame[1:2] * gain) / population
    cross = group_sum(frame[0:1] * gain) / population

    @pl.loop(0, slots)
    def _(r):
        grad = inverse * (up[span(r), :] * gain - delta - y1[span(r), :] * cross) * is_live(r)
        kept = grad.astype(BF16)
        grad = kept.astype(F32)
        g1[r] = kept
        g0[span(r), :] = earlier(grad).astype(BF16)
        g2[span(r), :] = later(grad).astype(BF16)

    hs2[0] = g1[0]
    hs2[1] = g1[jnp.clip(live - 1, 0, slots - 1)]
    halo_start(hs2, hr2, h2_s, h2_r)

    for b in range(3):
        right = g1[...].reshape(cells, chan) if b == 1 else (g0 if b == 0 else g2)[...]
        wide[...] = jnp.dot(xcat_t[...], right, preferred_element_type=F32)
        if aligned:
            for fi, p, low, size, tap, at in pieces:
                if tap % 3 == b:
                    a = tap // 3
                    dwbuf[fi, p // 2, p % 2, low:low + size, :] = wide[
                        a * chan + at:a * chan + at + size, :
                    ].astype(BF16)
        else:
            for a in range(3):
                dwf[(3 * a + b) * chan:(3 * a + b + 1) * chan, :] = wide[a * chan:(a + 1) * chan, :]
    for fi in range(shards):
        for p in range(tiles):
            low, high = p * part, min(shard, (p + 1) * part)
            if high <= low:
                dwbuf[fi, p // 2, p % 2] = jnp.zeros((part, chan), BF16)
            elif not aligned:
                rows = dwf[fi * shard + low:fi * shard + high, :]
                if high - low < part:
                    rows = jnp.concatenate([rows, jnp.zeros((part - high + low, chan), F32)], axis=0)
                dwbuf[fi, p // 2, p % 2] = rows.astype(BF16)
            elif high - low < part:
                dwbuf[fi, p // 2, p % 2, high - low:part, :] = jnp.zeros((part - high + low, chan), BF16)

    order = list(range(1, shards)) + [0]
    for k in order:
        fd = lax.rem(f + k, shards)
        push(dwbuf.at[fd, :, 1 - c], sbuf.at[k], b_s.at[k], b_r.at[k], sibling, f)
    for k in order:
        fd = lax.rem(f + k, shards)
        copy(sbuf.at[k], sbuf.at[k], b_s.at[k], b_r.at[k], sibling, f).wait_recv()
        for j in range(1, chips):
            to = peer_chip(j)
            pbuf[k, j - 1] = (dwbuf[fd, to, c].astype(F32) + sbuf[k, to].astype(F32)).astype(BF16)
            push(pbuf.at[k, j - 1], qbuf.at[k, j - 1], q_s.at[k, j - 1], q_r.at[k, j - 1], to * 2 + c, f)

    halo_wait(hs2, hr2, h2_s, h2_r)
    grad_below = hr2[1].astype(F32)
    for j in range(slots + 2):
        if j == 0:
            flat = hr2[0]
        elif j <= slots:
            flat = (g1[j - 1].astype(F32) + grad_below * is_end(j - 1)).astype(BF16)
        else:
            flat = (grad_below * is_end(slots)).astype(BF16)
        for a in range(3):
            r = j - 2 + a
            if 0 <= r < slots:
                cat[r * cols:(r + 1) * cols, a * chan:(a + 1) * chan] = flat
    three(cat, wt, (2, 1, 0))

    @pl.loop(0, slots)
    def _(r):
        rows = y1[span(r), :] + later(y0[span(r), :]) + earlier(y2[span(r), :])
        ig_ref[r] = (rows * is_live(r)).astype(BF16)

    own = None
    for k in order:
        fd = lax.rem(f + k, shards)
        summed = dwbuf[fd, ch, c].astype(F32) + sbuf[k, ch].astype(F32)
        for j in range(1, chips):
            block = qbuf.at[k, j - 1]
            copy(block, block, q_s.at[k, j - 1], q_r.at[k, j - 1], t, f).wait_recv()
            summed = summed + qbuf[k, j - 1].astype(F32)
        if k == 0:
            own = summed
        else:
            zbuf[k - 1] = summed.astype(BF16)
            push(zbuf.at[k - 1], rbuf.at[k - 1], r_s.at[k - 1], r_r.at[k - 1], t, fd)
    for k in range(1, shards):
        block = rbuf.at[k - 1]
        copy(block, block, r_s.at[k - 1], r_r.at[k - 1], t, f).wait_recv()
        own = own + rbuf[k - 1].astype(F32)
    fbuf[t] = own.astype(BF16)
    mine = fbuf.at[t]
    for j in range(1, chips):
        push(mine, mine, f_s.at[j - 1], f_r.at[j - 1], peer_chip(j) * 2 + c, f)
    push(mine, mine, e_s.at[0], e_r.at[0], sibling, f)

    scale = float(shards * ROWS_MEAN * tiles * cols) ** (-0.5)
    for k in range(1, shards):
        block = sz.at[lax.rem(f + shards - k, shards)]
        copy(block, block, sz_s.at[k - 1], sz_r.at[k - 1], t, f).wait_recv()
    every = sz[0]
    for i in range(1, shards):
        every = every + sz[i]
    gg_ref[...] = every[0:1] * scale
    bg_ref[...] = every[1:2] * scale

    for j in range(1, chips):
        block = fbuf.at[from_chip(j) * 2 + c]
        copy(block, block, f_s.at[j - 1], f_r.at[j - 1], t, f).wait_recv()
        push(block, block, e_s.at[j], e_r.at[j], sibling, f)
    for j in range(chips):
        block = fbuf.at[from_chip(j) * 2 + (1 - c)]
        copy(block, block, e_s.at[j], e_r.at[j], sibling, f).wait_recv()

    for p in range(-(-shard // part)):
        low, high = p * part, min(shard, (p + 1) * part)
        at = slice(low, high)
        grad = fbuf[p].astype(F32)[:high - low] * scale
        wg_ref[at, :] = grad
        first = 0.9 * m1_ref[at, :] + 0.1 * grad
        second = 0.999 * m2_ref[at, :] + 0.001 * grad * grad
        n1_ref[at, :] = first
        n2_ref[at, :] = second
        first_fix = first / (1.0 - 0.9**10)
        second_fix = second / (1.0 - 0.999**10)
        nw_ref[at, :] = w_ref[at, :] - 0.01 * first_fix / (jnp.sqrt(second_fix) + 1e-08)

    for made in sent:
        made.wait_send()


def local(
    images, tile_rows, cotangent, master_weight, norm_gain, norm_bias, first_moment, second_moment
):
    slots, cols, chan = images.shape[2:]
    cells = slots * cols
    shard = master_weight.shape[0]
    tiles = lax.axis_size("tile")
    shards = lax.axis_size("fsdp")
    chips = tiles // 2
    part = -(-shard // (tiles * 16)) * 16
    group = jnp.arange(chan) // (chan // GROUPS)
    same = (group[:, None] == group[None, :]).astype(F32)
    vmem = pl.BlockSpec(memory_space=pltpu.VMEM)
    dma = pltpu.SemaphoreType.DMA
    aligned = shard % 16 == 0
    rows_out = jax.ShapeDtypeStruct((shard, chan), F32)
    pair = [dma((2,))] * 2
    picture = jax.ShapeDtypeStruct((slots, cols, chan), BF16)
    line = jax.ShapeDtypeStruct((1, chan), F32)
    flops = 3 * 2 * cells * 9 * chan * chan
    result = pl.pallas_call(
        functools.partial(kernel, tiles, shards, part),
        out_shape=(picture, picture, rows_out, rows_out, rows_out, rows_out, line, line),
        in_specs=[pl.BlockSpec(memory_space=pltpu.SMEM)] + [vmem] * 8,
        out_specs=(vmem,) * 8,
        scratch_shapes=[
            pltpu.VMEM((shards, tiles, part, chan), BF16),
            pltpu.VMEM((3, 3 * chan, chan), BF16),
            pltpu.VMEM((3, 3 * chan, chan), BF16),
            pltpu.VMEM((3 * chan, chan), F32),
            pltpu.VMEM((cells, 3 * chan), BF16),
            pltpu.VMEM((3 * chan, cells), BF16),
            pltpu.VMEM((cells, 3 * chan), BF16),
            pltpu.VMEM((cells, chan), F32),
            pltpu.VMEM((cells, chan), F32),
            pltpu.VMEM((cells, chan), F32),
            pltpu.VMEM((cells, chan), F32),
            pltpu.VMEM((cells, chan), BF16),
            pltpu.VMEM((slots, cols, chan), BF16),
            pltpu.VMEM((cells, chan), BF16),
            pltpu.VMEM((2, cols, chan), BF16),
            pltpu.VMEM((2, cols, chan), BF16),
            pltpu.VMEM((2, cols, chan), BF16),
            pltpu.VMEM((2, cols, chan), BF16),
            pltpu.VMEM((tiles, 8, chan), F32),
            pltpu.VMEM((tiles, 8, chan), F32),
            pltpu.VMEM((shards, 8, chan), F32),
            pltpu.VMEM((shards, chips, 2, part, chan), BF16),
            pltpu.VMEM((8 if aligned else shards * shard, chan), F32),
            pltpu.VMEM((shards, chips, part, chan), BF16),
            pltpu.VMEM((shards, chips - 1, part, chan), BF16),
            pltpu.VMEM((shards, chips - 1, part, chan), BF16),
            pltpu.VMEM((shards - 1, part, chan), BF16),
            pltpu.VMEM((shards - 1, part, chan), BF16),
            pltpu.VMEM((tiles, part, chan), BF16),
            dma((shards - 1,)), dma((shards - 1,)),
            dma((shards - 1, chips - 1)), dma((shards - 1, chips - 1)),
            dma((shards - 1, chips)), dma((shards - 1, chips)),
            *pair, *pair,
            dma((tiles - 1,)), dma((tiles - 1,)),
            dma((tiles - 1,)), dma((tiles - 1,)),
            dma((shards - 1,)), dma((shards - 1,)),
            dma((shards,)), dma((shards,)),
            dma((shards, chips - 1)), dma((shards, chips - 1)),
            dma((shards - 1,)), dma((shards - 1,)),
            dma((chips - 1,)), dma((chips - 1,)),
            dma((chips,)), dma((chips,)),
        ],
        compiler_params=pltpu.CompilerParams(
            collective_id=0, has_side_effects=True, vmem_limit_bytes=58 * 2**20
        ),
        cost_estimate=pl.CostEstimate(
            flops=flops, bytes_accessed=16 * 2**20, transcendentals=cells * chan
        ),
        name="conv_block",
    )(
        tile_rows, images[0, 0], cotangent[0, 0], master_weight,
        norm_gain[None], norm_bias[None], first_moment, second_moment, same,
    )
    act, ig, wg, nw, n1, n2, gg, bg = result
    return (act.reshape(images.shape), ig.reshape(images.shape), wg, nw, n1, n2, gg[0], bg[0])


def solution(mesh):
    tiled = P("fsdp", "tile", None, None, None)
    rows = P("fsdp", None)
    return jax.shard_map(
        local,
        mesh=mesh,
        in_specs=(tiled, P("fsdp", "tile"), tiled, rows, P(), P(), rows, rows),
        out_specs=(tiled, tiled, rows, rows, rows, rows, P(), P()),
        check_vma=False,
    )
```

```python
import functools

import jax
import jax.numpy as jnp
from jax import lax
from jax.experimental import pallas as pl
from jax.experimental.pallas import tpu as pltpu
from jax.sharding import PartitionSpec as P

GROUPS = 32
ROWS_MEAN = 5
MESH = pl.DeviceIdType.MESH
F32 = jnp.float32
BF16 = jnp.bfloat16


def row_pieces(total, shards, shard, part, block):
    found = []
    for f in range(shards):
        for p in range(-(-shard // part)):
            low, high = f * shard + p * part, f * shard + min(shard, (p + 1) * part)
            at = low
            while at < high:
                end = min(high, (at // block + 1) * block)
                found.append((f, p, at - low, end - at, at // block, at % block))
                at = end
    return found


def kernel(
    tiles, shards, part,
    rows_ref, x_ref, ct_any, w_ref, gain_ref, bias_ref, m1_any, m2_any,
    act_any, ig_any, wg_ref, nw_ref, n1_ref, n2_ref, gg_ref, bg_ref,
    ct_ref, m1_ref, m2_ref, act_ref, ig_ref, same_ref, wrow, loc,
    gath, wb, wt, wide, xcat, xcat_t, cat, y0, y1, y2, up, g0, g1, g2,
    hs, hr, hs2, hr2, st, sd, sz,
    dwbuf, dwf, sbuf, pbuf, qbuf, zbuf, rbuf, fbuf,
    z_s, z_r, p_s, p_r, s_s, s_r, h_s, h_r, h2_s, h2_r, st_s, st_r, sd_s, sd_r, sz_s, sz_r,
    b_s, b_r, q_s, q_r, r_s, r_r, f_s, f_r, e_s, e_r,
):
    slots, chan, cols = x_ref.shape
    cells = slots * cols
    shard = w_ref.shape[1]
    total = shards * shard
    chips = tiles // 2
    t = lax.axis_index("tile")
    f = lax.axis_index("fsdp")
    ch, c = t // 2, t % 2
    sibling = ch * 2 + (1 - c)
    live = rows_ref[0, 0]
    aligned = shard % 16 == 0
    sent = []

    def peer_chip(j):
        return lax.rem(ch + j, chips)

    def from_chip(j):
        return lax.rem(ch + chips - j, chips)

    def copy(src, dst, send, recv, to_tile, to_shard):
        return pltpu.make_async_remote_copy(
            src_ref=src, dst_ref=dst, send_sem=send, recv_sem=recv,
            device_id=(to_tile, to_shard), device_id_type=MESH,
        )

    def push(*args):
        made = copy(*args)
        made.start()
        sent.append(made)

    barrier = pltpu.get_barrier_semaphore()
    for j in range(1, tiles):
        pl.semaphore_signal(barrier, inc=1, device_id=(lax.rem(t + j, tiles), f), device_id_type=MESH)
    for k in range(1, shards):
        pl.semaphore_signal(barrier, inc=1, device_id=(t, lax.rem(f + k, shards)), device_id_type=MESH)

    loads = [
        pltpu.make_async_copy(src, dst, loc.at[i])
        for i, (src, dst) in enumerate(((ct_any, ct_ref), (m1_any, m1_ref), (m2_any, m2_ref)))
    ]
    for load in loads:
        load.start()

    wrow[...] = w_ref[...].T
    for p in range(tiles):
        low, high = p * part, min(shard, (p + 1) * part)
        if high <= low:
            gath[f, p] = jnp.zeros((part, chan), BF16)
        else:
            rows = wrow[low:high, :]
            if high - low < part:
                rows = jnp.concatenate([rows, jnp.zeros((part - high + low, chan), F32)], axis=0)
            gath[f, p] = rows.astype(BF16)
    hs[0] = x_ref[0]
    hs[1] = x_ref[jnp.clip(live - 1, 0, slots - 1)]
    pl.semaphore_wait(barrier, tiles + shards - 2)

    for k in range(1, shards):
        push(gath.at[f, t], gath.at[f, t], z_s.at[k - 1], z_r.at[k - 1], t, lax.rem(f + k, shards))

    def halo_copies(src, dst, send, recv):
        up_copy = copy(src.at[0], dst.at[1], send.at[0], recv.at[1], lax.rem(t + tiles - 1, tiles), f)
        down_copy = copy(src.at[1], dst.at[0], send.at[1], recv.at[0], lax.rem(t + 1, tiles), f)
        return up_copy, down_copy

    def halo_start(src, dst, send, recv):
        up_copy, down_copy = halo_copies(src, dst, send, recv)

        @pl.when(t > 0)
        def _():
            up_copy.start()

        @pl.when(t == 0)
        def _():
            dst[0] = jnp.zeros(dst.shape[1:], BF16)

        @pl.when(t < tiles - 1)
        def _():
            down_copy.start()

        @pl.when(t == tiles - 1)
        def _():
            dst[1] = jnp.zeros(dst.shape[1:], BF16)

    def halo_wait(src, dst, send, recv):
        up_copy, down_copy = halo_copies(src, dst, send, recv)

        @pl.when(t > 0)
        def _():
            up_copy.wait_send()
            down_copy.wait_recv()

        @pl.when(t < tiles - 1)
        def _():
            down_copy.wait_send()
            up_copy.wait_recv()

    halo_start(hs, hr, h_s, h_r)

    for k in range(1, shards):
        fs = lax.rem(f + shards - k, shards)
        block = gath.at[fs, t]
        copy(block, block, z_s.at[k - 1], z_r.at[k - 1], t, f).wait_recv()
        for j in range(1, chips):
            push(block, block, p_s.at[k - 1, j - 1], p_r.at[k - 1, j - 1], peer_chip(j) * 2 + c, f)
        push(block, block, s_s.at[k - 1, 0], s_r.at[k - 1, 0], sibling, f)

    halo_wait(hs, hr, h_s, h_r)
    below = hr[1].astype(F32)

    def is_live(r):
        return (r < live).astype(F32)

    def is_end(r):
        return (r == live).astype(F32)

    for j in range(slots + 2):
        if j == 0:
            value = hr[0].astype(F32)
        elif j <= slots:
            value = x_ref[j - 1].astype(F32) * is_live(j - 1) + below * is_end(j - 1)
        else:
            value = below * is_end(slots)
        flat, turned = value.T.astype(BF16), value.astype(BF16)
        for a in range(3):
            r = j - a
            if 0 <= r < slots:
                xcat[r * cols:(r + 1) * cols, a * chan:(a + 1) * chan] = flat
                xcat_t[a * chan:(a + 1) * chan, r * cols:(r + 1) * cols] = turned

    loads[0].wait()
    for r in range(slots):
        up[r * cols:(r + 1) * cols, :] = ct_ref[r].astype(F32).T
    across = lax.broadcasted_iota(jnp.int32, (chan, chan), 1).astype(F32)
    down = lax.broadcasted_iota(jnp.int32, (chan, chan), 0).astype(F32)
    per = float(chan // GROUPS)
    same_ref[...] = (jnp.floor((across + 0.5) / per) == jnp.floor((down + 0.5) / per)).astype(F32)

    for k in range(1, shards):
        fs = lax.rem(f + shards - k, shards)
        for j in range(1, chips):
            block = gath.at[fs, from_chip(j) * 2 + c]
            copy(block, block, p_s.at[k - 1, j - 1], p_r.at[k - 1, j - 1], t, f).wait_recv()
            push(block, block, s_s.at[k - 1, j], s_r.at[k - 1, j], sibling, f)
    for k in range(1, shards):
        fs = lax.rem(f + shards - k, shards)
        for j in range(chips):
            block = gath.at[fs, from_chip(j) * 2 + (1 - c)]
            copy(block, block, s_s.at[k - 1, j], s_r.at[k - 1, j], sibling, f).wait_recv()

    pieces = row_pieces(total, shards, shard, part, chan)
    if aligned:
        for fi, p, low, size, tap, at in pieces:
            a, b = tap // 3, tap % 3
            wb[b, a * chan + at:a * chan + at + size, :] = gath[fi, p, low:low + size, :]
    else:
        for fi in range(shards):
            for p in range(-(-shard // part)):
                size = min(shard - p * part, part)
                dwf[fi * shard + p * part:fi * shard + p * part + size, :] = (
                    gath[fi, p].astype(F32)[:size]
                )
        for tap in range(9):
            a, b = tap // 3, tap % 3
            wb[b, a * chan:(a + 1) * chan, :] = dwf[tap * chan:(tap + 1) * chan, :].astype(BF16)

    half = cells // 2

    def three(source, weights, order):
        @pl.loop(0, 2)
        def _(h):
            at = pl.ds(pl.multiple_of(h * half, half), half)
            left = source[at, :]
            for b, into in zip(order, (y0, y1, y2)):
                into[at, :] = jnp.dot(left, weights[b], preferred_element_type=F32)

    column = lax.broadcasted_iota(jnp.int32, (cols, chan), 0)

    def later(rows):
        return jnp.where(column == 0, 0.0, pltpu.roll(rows, 1, 0))

    def earlier(rows):
        return jnp.where(column == cols - 1, 0.0, pltpu.roll(rows, cols - 1, 0))

    def span(r):
        return pl.ds(pl.multiple_of(r * cols, cols), cols)

    def group_sum(row):
        return jnp.dot(row, same_ref[...], precision=lax.Precision.HIGHEST, preferred_element_type=F32)

    three(xcat, wb, (0, 1, 2))

    def mix(r, sums):
        rows = y1[span(r), :] + later(y0[span(r), :]) + earlier(y2[span(r), :])
        y1[span(r), :] = rows
        return sums + jnp.sum(rows, axis=0, keepdims=True) * is_live(r)

    zero_row = jnp.zeros((1, chan), F32)
    own_count = live.astype(F32) * (cols * (chan // GROUPS))
    count_row = jnp.zeros((1, chan), F32) + own_count
    own_mean = group_sum(lax.fori_loop(0, slots, mix, zero_row)) / count_row

    def squares(r, sums):
        off = y1[span(r), :] - own_mean
        return sums + jnp.sum(off * off, axis=0, keepdims=True) * is_live(r)

    own_square = group_sum(lax.fori_loop(0, slots, squares, zero_row))

    def tile_share(buffer, send, recv):
        for j in range(1, tiles):
            push(buffer.at[t], buffer.at[t], send.at[j - 1], recv.at[j - 1], lax.rem(t + j, tiles), f)

    def tile_wait(buffer, send, recv):
        for j in range(1, tiles):
            block = buffer.at[lax.rem(t + tiles - j, tiles)]
            copy(block, block, send.at[j - 1], recv.at[j - 1], t, f).wait_recv()

    st[t] = jnp.concatenate(
        [own_mean, own_square, count_row, jnp.zeros((5, chan), F32)], axis=0
    )
    tile_share(st, st_s, st_r)

    for tap in range(9):
        a, b = tap // 3, tap % 3
        block = wb[b, a * chan:(a + 1) * chan, :].astype(F32)
        wt[b, a * chan:(a + 1) * chan, :] = block.T.astype(BF16)

    tile_wait(st, st_s, st_r)
    population = float(ROWS_MEAN * tiles * cols * (chan // GROUPS))
    mean = zero_row
    for i in range(tiles):
        mean = mean + st[i, 0:1, :] * st[i, 2:3, :]
    mean = mean / population
    spread = zero_row
    for i in range(tiles):
        apart = st[i, 0:1, :] - mean
        spread = spread + st[i, 1:2, :] + st[i, 2:3, :] * apart * apart
    inverse = lax.rsqrt(spread / population + 1e-05)
    gain, bias = gain_ref[...].reshape(1, chan), bias_ref[...].reshape(1, chan)

    def gate(r, sums):
        gains, biases = sums
        mask = is_live(r)
        normed = (y1[span(r), :] - mean) * inverse
        shifted = normed * gain + bias
        s = jax.nn.sigmoid(shifted)
        act_ref[r] = (shifted * s * mask).T.astype(BF16)
        dshift = up[span(r), :] * mask * s * (1.0 + shifted * (1.0 - s))
        y1[span(r), :] = normed
        up[span(r), :] = dshift
        return (
            gains + jnp.sum(dshift * normed, axis=0, keepdims=True),
            biases + jnp.sum(dshift, axis=0, keepdims=True),
        )

    own_gain, own_bias = lax.fori_loop(0, slots, gate, (zero_row, zero_row))
    act_out = pltpu.make_async_copy(act_ref, act_any, loc.at[3])
    act_out.start()
    sd[t] = jnp.concatenate([own_gain, own_bias, jnp.zeros((6, chan), F32)], axis=0)
    tile_share(sd, sd_s, sd_r)
    tile_wait(sd, sd_s, sd_r)
    frame = sd[0]
    for i in range(1, tiles):
        frame = frame + sd[i]
    sz[f] = frame
    for k in range(1, shards):
        push(sz.at[f], sz.at[f], sz_s.at[k - 1], sz_r.at[k - 1], t, lax.rem(f + k, shards))
    delta = group_sum(frame[1:2] * gain) / population
    cross = group_sum(frame[0:1] * gain) / population

    @pl.loop(0, slots)
    def _(r):
        grad = inverse * (up[span(r), :] * gain - delta - y1[span(r), :] * cross) * is_live(r)
        kept = grad.astype(BF16)
        grad = kept.astype(F32)
        g1[r] = kept
        g0[span(r), :] = earlier(grad).astype(BF16)
        g2[span(r), :] = later(grad).astype(BF16)

    hs2[0] = g1[0]
    hs2[1] = g1[jnp.clip(live - 1, 0, slots - 1)]
    halo_start(hs2, hr2, h2_s, h2_r)

    for b in range(3):
        right = g1[...].reshape(cells, chan) if b == 1 else (g0 if b == 0 else g2)[...]
        wide[...] = jnp.dot(xcat_t[...], right, preferred_element_type=F32)
        if aligned:
            for fi, p, low, size, tap, at in pieces:
                if tap % 3 == b:
                    a = tap // 3
                    dwbuf[fi, p // 2, p % 2, low:low + size, :] = wide[
                        a * chan + at:a * chan + at + size, :
                    ].astype(BF16)
        else:
            for a in range(3):
                dwf[(3 * a + b) * chan:(3 * a + b + 1) * chan, :] = wide[a * chan:(a + 1) * chan, :]
    for fi in range(shards):
        for p in range(tiles):
            low, high = p * part, min(shard, (p + 1) * part)
            if high <= low:
                dwbuf[fi, p // 2, p % 2] = jnp.zeros((part, chan), BF16)
            elif not aligned:
                rows = dwf[fi * shard + low:fi * shard + high, :]
                if high - low < part:
                    rows = jnp.concatenate([rows, jnp.zeros((part - high + low, chan), F32)], axis=0)
                dwbuf[fi, p // 2, p % 2] = rows.astype(BF16)
            elif high - low < part:
                dwbuf[fi, p // 2, p % 2, high - low:part, :] = jnp.zeros((part - high + low, chan), BF16)

    order = list(range(1, shards)) + [0]
    for k in order:
        fd = lax.rem(f + k, shards)
        push(dwbuf.at[fd, :, 1 - c], sbuf.at[k], b_s.at[k], b_r.at[k], sibling, f)
    for k in order:
        fd = lax.rem(f + k, shards)
        copy(sbuf.at[k], sbuf.at[k], b_s.at[k], b_r.at[k], sibling, f).wait_recv()
        for j in range(1, chips):
            to = peer_chip(j)
            pbuf[k, j - 1] = (dwbuf[fd, to, c].astype(F32) + sbuf[k, to].astype(F32)).astype(BF16)
            push(pbuf.at[k, j - 1], qbuf.at[k, j - 1], q_s.at[k, j - 1], q_r.at[k, j - 1], to * 2 + c, f)

    halo_wait(hs2, hr2, h2_s, h2_r)
    grad_below = hr2[1].astype(F32)
    for j in range(slots + 2):
        if j == 0:
            flat = hr2[0]
        elif j <= slots:
            flat = (g1[j - 1].astype(F32) + grad_below * is_end(j - 1)).astype(BF16)
        else:
            flat = (grad_below * is_end(slots)).astype(BF16)
        for a in range(3):
            r = j - 2 + a
            if 0 <= r < slots:
                cat[r * cols:(r + 1) * cols, a * chan:(a + 1) * chan] = flat
    three(cat, wt, (2, 1, 0))

    @pl.loop(0, slots)
    def _(r):
        rows = y1[span(r), :] + later(y0[span(r), :]) + earlier(y2[span(r), :])
        ig_ref[r] = (rows * is_live(r)).T.astype(BF16)

    ig_out = pltpu.make_async_copy(ig_ref, ig_any, loc.at[4])
    ig_out.start()

    own = None
    for k in order:
        fd = lax.rem(f + k, shards)
        summed = dwbuf[fd, ch, c].astype(F32) + sbuf[k, ch].astype(F32)
        for j in range(1, chips):
            block = qbuf.at[k, j - 1]
            copy(block, block, q_s.at[k, j - 1], q_r.at[k, j - 1], t, f).wait_recv()
            summed = summed + qbuf[k, j - 1].astype(F32)
        if k == 0:
            own = summed
        else:
            zbuf[k - 1] = summed.astype(BF16)
            push(zbuf.at[k - 1], rbuf.at[k - 1], r_s.at[k - 1], r_r.at[k - 1], t, fd)
    for k in range(1, shards):
        block = rbuf.at[k - 1]
        copy(block, block, r_s.at[k - 1], r_r.at[k - 1], t, f).wait_recv()
        own = own + rbuf[k - 1].astype(F32)
    fbuf[t] = own.astype(BF16)
    mine = fbuf.at[t]
    for j in range(1, chips):
        push(mine, mine, f_s.at[j - 1], f_r.at[j - 1], peer_chip(j) * 2 + c, f)
    push(mine, mine, e_s.at[0], e_r.at[0], sibling, f)

    scale = float(shards * ROWS_MEAN * tiles * cols) ** (-0.5)
    for k in range(1, shards):
        block = sz.at[lax.rem(f + shards - k, shards)]
        copy(block, block, sz_s.at[k - 1], sz_r.at[k - 1], t, f).wait_recv()
    every = sz[0]
    for i in range(1, shards):
        every = every + sz[i]
    gg_ref[...] = (every[0:1] * scale).reshape(chan)
    bg_ref[...] = (every[1:2] * scale).reshape(chan)

    for j in range(1, chips):
        block = fbuf.at[from_chip(j) * 2 + c]
        copy(block, block, f_s.at[j - 1], f_r.at[j - 1], t, f).wait_recv()
        push(block, block, e_s.at[j], e_r.at[j], sibling, f)
    for j in range(chips):
        block = fbuf.at[from_chip(j) * 2 + (1 - c)]
        copy(block, block, e_s.at[j], e_r.at[j], sibling, f).wait_recv()

    for p in range(-(-shard // part)):
        low, high = p * part, min(shard, (p + 1) * part)
        wrow[low:high, :] = fbuf[p].astype(F32)[:high - low]
    loads[1].wait()
    loads[2].wait()
    grad = wrow[...].T * scale
    wg_ref[...] = grad
    first = 0.9 * m1_ref[...] + 0.1 * grad
    second = 0.999 * m2_ref[...] + 0.001 * grad * grad
    n1_ref[...] = first
    n2_ref[...] = second
    first_fix = first / (1.0 - 0.9**10)
    second_fix = second / (1.0 - 0.999**10)
    nw_ref[...] = w_ref[...] - 0.01 * first_fix / (jnp.sqrt(second_fix) + 1e-08)

    act_out.wait()
    ig_out.wait()
    for made in sent:
        made.wait_send()


def swapped(array):
    return jnp.swapaxes(array, 1, 2)


def local(
    images, tile_rows, cotangent, master_weight, norm_gain, norm_bias, first_moment, second_moment
):
    slots, cols, chan = images.shape[2:]
    cells = slots * cols
    shard = master_weight.shape[0]
    tiles = lax.axis_size("tile")
    shards = lax.axis_size("fsdp")
    chips = tiles // 2
    part = -(-shard // (tiles * 16)) * 16
    anywhere = pl.BlockSpec(memory_space=pl.ANY)
    vmem = pl.BlockSpec(memory_space=pltpu.VMEM)
    dma = pltpu.SemaphoreType.DMA
    aligned = shard % 16 == 0
    rows_out = jax.ShapeDtypeStruct((chan, shard), F32)
    pair = [dma((2,))] * 2
    picture = jax.ShapeDtypeStruct((slots, chan, cols), BF16)
    line = jax.ShapeDtypeStruct((chan,), F32)
    flops = 3 * 2 * cells * 9 * chan * chan
    result = pl.pallas_call(
        functools.partial(kernel, tiles, shards, part),
        out_shape=(picture, picture, rows_out, rows_out, rows_out, rows_out, line, line),
        in_specs=[
            pl.BlockSpec(memory_space=pltpu.SMEM), vmem, anywhere, vmem, vmem, vmem, anywhere, anywhere
        ],
        out_specs=(anywhere, anywhere) + (vmem,) * 6,
        scratch_shapes=[
            pltpu.VMEM((slots, chan, cols), BF16),
            pltpu.VMEM((chan, shard), F32),
            pltpu.VMEM((chan, shard), F32),
            pltpu.VMEM((slots, chan, cols), BF16),
            pltpu.VMEM((slots, chan, cols), BF16),
            pltpu.VMEM((chan, chan), F32),
            pltpu.VMEM((shard, chan), F32),
            dma((5,)),
            pltpu.VMEM((shards, tiles, part, chan), BF16),
            pltpu.VMEM((3, 3 * chan, chan), BF16),
            pltpu.VMEM((3, 3 * chan, chan), BF16),
            pltpu.VMEM((3 * chan, chan), F32),
            pltpu.VMEM((cells, 3 * chan), BF16),
            pltpu.VMEM((3 * chan, cells), BF16),
            pltpu.VMEM((cells, 3 * chan), BF16),
            pltpu.VMEM((cells, chan), F32),
            pltpu.VMEM((cells, chan), F32),
            pltpu.VMEM((cells, chan), F32),
            pltpu.VMEM((cells, chan), F32),
            pltpu.VMEM((cells, chan), BF16),
            pltpu.VMEM((slots, cols, chan), BF16),
            pltpu.VMEM((cells, chan), BF16),
            pltpu.VMEM((2, chan, cols), BF16),
            pltpu.VMEM((2, chan, cols), BF16),
            pltpu.VMEM((2, cols, chan), BF16),
            pltpu.VMEM((2, cols, chan), BF16),
            pltpu.VMEM((tiles, 8, chan), F32),
            pltpu.VMEM((tiles, 8, chan), F32),
            pltpu.VMEM((shards, 8, chan), F32),
            pltpu.VMEM((shards, chips, 2, part, chan), BF16),
            pltpu.VMEM((8 if aligned else shards * shard, chan), F32),
            pltpu.VMEM((shards, chips, part, chan), BF16),
            pltpu.VMEM((shards, chips - 1, part, chan), BF16),
            pltpu.VMEM((shards, chips - 1, part, chan), BF16),
            pltpu.VMEM((shards - 1, part, chan), BF16),
            pltpu.VMEM((shards - 1, part, chan), BF16),
            pltpu.VMEM((tiles, part, chan), BF16),
            dma((shards - 1,)), dma((shards - 1,)),
            dma((shards - 1, chips - 1)), dma((shards - 1, chips - 1)),
            dma((shards - 1, chips)), dma((shards - 1, chips)),
            *pair, *pair,
            dma((tiles - 1,)), dma((tiles - 1,)),
            dma((tiles - 1,)), dma((tiles - 1,)),
            dma((shards - 1,)), dma((shards - 1,)),
            dma((shards,)), dma((shards,)),
            dma((shards, chips - 1)), dma((shards, chips - 1)),
            dma((shards - 1,)), dma((shards - 1,)),
            dma((chips - 1,)), dma((chips - 1,)),
            dma((chips,)), dma((chips,)),
        ],
        compiler_params=pltpu.CompilerParams(
            collective_id=0, has_side_effects=True, vmem_limit_bytes=58 * 2**20
        ),
        cost_estimate=pl.CostEstimate(
            flops=flops, bytes_accessed=16 * 2**20, transcendentals=cells * chan
        ),
        name="conv_block",
    )(
        tile_rows, swapped(images[0, 0]), swapped(cotangent[0, 0]), master_weight.T,
        norm_gain, norm_bias, first_moment.T, second_moment.T,
    )
    act, ig, wg, nw, n1, n2, gg, bg = result
    act, ig = swapped(act).reshape(images.shape), swapped(ig).reshape(images.shape)
    return (act, ig, wg.T, nw.T, n1.T, n2.T, gg, bg)


def solution(mesh):
    tiled = P("fsdp", "tile", None, None, None)
    rows = P("fsdp", None)
    return jax.shard_map(
        local,
        mesh=mesh,
        in_specs=(tiled, P("fsdp", "tile"), tiled, rows, P(), P(), rows, rows),
        out_specs=(tiled, tiled, rows, rows, rows, rows, P(), P()),
        check_vma=False,
    )
```

```python
import functools

import jax
import jax.numpy as jnp
from jax import lax
from jax.experimental import pallas as pl
from jax.experimental.pallas import tpu as pltpu
from jax.sharding import PartitionSpec as P

GROUPS = 32
ROWS_MEAN = 5
MESH = pl.DeviceIdType.MESH
F32 = jnp.float32
BF16 = jnp.bfloat16


def row_pieces(total, shards, shard, part, block):
    found = []
    for f in range(shards):
        for p in range(-(-shard // part)):
            low, high = f * shard + p * part, f * shard + min(shard, (p + 1) * part)
            at = low
            while at < high:
                end = min(high, (at // block + 1) * block)
                found.append((f, p, at - low, end - at, at // block, at % block))
                at = end
    return found


def kernel(
    tiles, shards, part,
    rows_ref, x_ref, ct_any, w_ref, gain_ref, bias_ref,
    act_any, ig_any, wg_ref, gg_ref, bg_ref,
    ct_ref, act_ref, ig_ref, same_ref, wrow, loc,
    gath, wb, wt, wide, xcat, xcat_t, cat, y0, y1, y2, up, g0, g1, g2,
    hs, hr, hs2, hr2, st, sd, sz,
    dwbuf, dwf, sbuf, pbuf, qbuf, zbuf, rbuf, fbuf,
    z_s, z_r, p_s, p_r, s_s, s_r, h_s, h_r, h2_s, h2_r, st_s, st_r, sd_s, sd_r, sz_s, sz_r,
    b_s, b_r, q_s, q_r, r_s, r_r, f_s, f_r, e_s, e_r,
):
    slots, chan, cols = x_ref.shape
    cells = slots * cols
    shard = w_ref.shape[1]
    total = shards * shard
    chips = tiles // 2
    t = lax.axis_index("tile")
    f = lax.axis_index("fsdp")
    ch, c = t // 2, t % 2
    sibling = ch * 2 + (1 - c)
    live = rows_ref[0, 0]
    aligned = shard % 16 == 0
    sent = []

    def peer_chip(j):
        return lax.rem(ch + j, chips)

    def from_chip(j):
        return lax.rem(ch + chips - j, chips)

    def copy(src, dst, send, recv, to_tile, to_shard):
        return pltpu.make_async_remote_copy(
            src_ref=src, dst_ref=dst, send_sem=send, recv_sem=recv,
            device_id=(to_tile, to_shard), device_id_type=MESH,
        )

    def push(*args):
        made = copy(*args)
        made.start()
        sent.append(made)

    barrier = pltpu.get_barrier_semaphore()
    for j in range(1, tiles):
        pl.semaphore_signal(barrier, inc=1, device_id=(lax.rem(t + j, tiles), f), device_id_type=MESH)
    for k in range(1, shards):
        pl.semaphore_signal(barrier, inc=1, device_id=(t, lax.rem(f + k, shards)), device_id_type=MESH)

    ct_in = pltpu.make_async_copy(ct_any, ct_ref, loc.at[0])
    ct_in.start()

    wrow[...] = w_ref[...].T
    for p in range(tiles):
        low, high = p * part, min(shard, (p + 1) * part)
        if high <= low:
            gath[f, p] = jnp.zeros((part, chan), BF16)
        else:
            rows = wrow[low:high, :]
            if high - low < part:
                rows = jnp.concatenate([rows, jnp.zeros((part - high + low, chan), F32)], axis=0)
            gath[f, p] = rows.astype(BF16)
    hs[0] = x_ref[0]
    hs[1] = x_ref[jnp.clip(live - 1, 0, slots - 1)]
    pl.semaphore_wait(barrier, tiles + shards - 2)

    for k in range(1, shards):
        push(gath.at[f, t], gath.at[f, t], z_s.at[k - 1], z_r.at[k - 1], t, lax.rem(f + k, shards))

    def halo_copies(src, dst, send, recv):
        up_copy = copy(src.at[0], dst.at[1], send.at[0], recv.at[1], lax.rem(t + tiles - 1, tiles), f)
        down_copy = copy(src.at[1], dst.at[0], send.at[1], recv.at[0], lax.rem(t + 1, tiles), f)
        return up_copy, down_copy

    def halo_start(src, dst, send, recv):
        up_copy, down_copy = halo_copies(src, dst, send, recv)

        @pl.when(t > 0)
        def _():
            up_copy.start()

        @pl.when(t == 0)
        def _():
            dst[0] = jnp.zeros(dst.shape[1:], BF16)

        @pl.when(t < tiles - 1)
        def _():
            down_copy.start()

        @pl.when(t == tiles - 1)
        def _():
            dst[1] = jnp.zeros(dst.shape[1:], BF16)

    def halo_wait(src, dst, send, recv):
        up_copy, down_copy = halo_copies(src, dst, send, recv)

        @pl.when(t > 0)
        def _():
            up_copy.wait_send()
            down_copy.wait_recv()

        @pl.when(t < tiles - 1)
        def _():
            down_copy.wait_send()
            up_copy.wait_recv()

    halo_start(hs, hr, h_s, h_r)

    for k in range(1, shards):
        fs = lax.rem(f + shards - k, shards)
        block = gath.at[fs, t]
        copy(block, block, z_s.at[k - 1], z_r.at[k - 1], t, f).wait_recv()
        for j in range(1, chips):
            push(block, block, p_s.at[k - 1, j - 1], p_r.at[k - 1, j - 1], peer_chip(j) * 2 + c, f)
        push(block, block, s_s.at[k - 1, 0], s_r.at[k - 1, 0], sibling, f)

    halo_wait(hs, hr, h_s, h_r)
    below = hr[1].astype(F32)

    def is_live(r):
        return (r < live).astype(F32)

    def is_end(r):
        return (r == live).astype(F32)

    for j in range(slots + 2):
        if j == 0:
            value = hr[0].astype(F32)
        elif j <= slots:
            value = x_ref[j - 1].astype(F32) * is_live(j - 1) + below * is_end(j - 1)
        else:
            value = below * is_end(slots)
        flat, turned = value.T.astype(BF16), value.astype(BF16)
        for a in range(3):
            r = j - a
            if 0 <= r < slots:
                xcat[r * cols:(r + 1) * cols, a * chan:(a + 1) * chan] = flat
                xcat_t[a * chan:(a + 1) * chan, r * cols:(r + 1) * cols] = turned

    ct_in.wait()
    for r in range(slots):
        up[r * cols:(r + 1) * cols, :] = ct_ref[r].astype(F32).T
    across = lax.broadcasted_iota(jnp.int32, (chan, chan), 1).astype(F32)
    down = lax.broadcasted_iota(jnp.int32, (chan, chan), 0).astype(F32)
    per = float(chan // GROUPS)
    same_ref[...] = (jnp.floor((across + 0.5) / per) == jnp.floor((down + 0.5) / per)).astype(F32)

    for k in range(1, shards):
        fs = lax.rem(f + shards - k, shards)
        for j in range(1, chips):
            block = gath.at[fs, from_chip(j) * 2 + c]
            copy(block, block, p_s.at[k - 1, j - 1], p_r.at[k - 1, j - 1], t, f).wait_recv()
            push(block, block, s_s.at[k - 1, j], s_r.at[k - 1, j], sibling, f)
    for k in range(1, shards):
        fs = lax.rem(f + shards - k, shards)
        for j in range(chips):
            block = gath.at[fs, from_chip(j) * 2 + (1 - c)]
            copy(block, block, s_s.at[k - 1, j], s_r.at[k - 1, j], sibling, f).wait_recv()

    pieces = row_pieces(total, shards, shard, part, chan)
    if aligned:
        for fi, p, low, size, tap, at in pieces:
            a, b = tap // 3, tap % 3
            wb[b, a * chan + at:a * chan + at + size, :] = gath[fi, p, low:low + size, :]
    else:
        for fi in range(shards):
            for p in range(-(-shard // part)):
                size = min(shard - p * part, part)
                dwf[fi * shard + p * part:fi * shard + p * part + size, :] = (
                    gath[fi, p].astype(F32)[:size]
                )
        for tap in range(9):
            a, b = tap // 3, tap % 3
            wb[b, a * chan:(a + 1) * chan, :] = dwf[tap * chan:(tap + 1) * chan, :].astype(BF16)

    half = cells // 2

    def three(source, weights, order):
        @pl.loop(0, 2)
        def _(h):
            at = pl.ds(pl.multiple_of(h * half, half), half)
            left = source[at, :]
            for b, into in zip(order, (y0, y1, y2)):
                into[at, :] = jnp.dot(left, weights[b], preferred_element_type=F32)

    column = lax.broadcasted_iota(jnp.int32, (cols, chan), 0)

    def later(rows):
        return jnp.where(column == 0, 0.0, pltpu.roll(rows, 1, 0))

    def earlier(rows):
        return jnp.where(column == cols - 1, 0.0, pltpu.roll(rows, cols - 1, 0))

    def span(r):
        return pl.ds(pl.multiple_of(r * cols, cols), cols)

    def group_sum(row):
        return jnp.dot(row, same_ref[...], precision=lax.Precision.HIGHEST, preferred_element_type=F32)

    three(xcat, wb, (0, 1, 2))

    def mix(r, sums):
        rows = y1[span(r), :] + later(y0[span(r), :]) + earlier(y2[span(r), :])
        y1[span(r), :] = rows
        return sums + jnp.sum(rows, axis=0, keepdims=True) * is_live(r)

    zero_row = jnp.zeros((1, chan), F32)
    own_count = live.astype(F32) * (cols * (chan // GROUPS))
    count_row = jnp.zeros((1, chan), F32) + own_count
    own_mean = group_sum(lax.fori_loop(0, slots, mix, zero_row)) / count_row

    def squares(r, sums):
        off = y1[span(r), :] - own_mean
        return sums + jnp.sum(off * off, axis=0, keepdims=True) * is_live(r)

    own_square = group_sum(lax.fori_loop(0, slots, squares, zero_row))

    def tile_share(buffer, send, recv):
        for j in range(1, tiles):
            push(buffer.at[t], buffer.at[t], send.at[j - 1], recv.at[j - 1], lax.rem(t + j, tiles), f)

    def tile_wait(buffer, send, recv):
        for j in range(1, tiles):
            block = buffer.at[lax.rem(t + tiles - j, tiles)]
            copy(block, block, send.at[j - 1], recv.at[j - 1], t, f).wait_recv()

    st[t] = jnp.concatenate(
        [own_mean, own_square, count_row, jnp.zeros((5, chan), F32)], axis=0
    )
    tile_share(st, st_s, st_r)

    for tap in range(9):
        a, b = tap // 3, tap % 3
        block = wb[b, a * chan:(a + 1) * chan, :].astype(F32)
        wt[b, a * chan:(a + 1) * chan, :] = block.T.astype(BF16)

    tile_wait(st, st_s, st_r)
    population = float(ROWS_MEAN * tiles * cols * (chan // GROUPS))
    mean = zero_row
    for i in range(tiles):
        mean = mean + st[i, 0:1, :] * st[i, 2:3, :]
    mean = mean / population
    spread = zero_row
    for i in range(tiles):
        apart = st[i, 0:1, :] - mean
        spread = spread + st[i, 1:2, :] + st[i, 2:3, :] * apart * apart
    inverse = lax.rsqrt(spread / population + 1e-05)
    gain, bias = gain_ref[...].reshape(1, chan), bias_ref[...].reshape(1, chan)

    def gate(r, sums):
        gains, biases = sums
        mask = is_live(r)
        normed = (y1[span(r), :] - mean) * inverse
        shifted = normed * gain + bias
        s = jax.nn.sigmoid(shifted)
        act_ref[r] = (shifted * s * mask).T.astype(BF16)
        dshift = up[span(r), :] * mask * s * (1.0 + shifted * (1.0 - s))
        y1[span(r), :] = normed
        up[span(r), :] = dshift
        return (
            gains + jnp.sum(dshift * normed, axis=0, keepdims=True),
            biases + jnp.sum(dshift, axis=0, keepdims=True),
        )

    own_gain, own_bias = lax.fori_loop(0, slots, gate, (zero_row, zero_row))
    act_out = pltpu.make_async_copy(act_ref, act_any, loc.at[1])
    act_out.start()
    sd[t] = jnp.concatenate([own_gain, own_bias, jnp.zeros((6, chan), F32)], axis=0)
    tile_share(sd, sd_s, sd_r)
    tile_wait(sd, sd_s, sd_r)
    frame = sd[0]
    for i in range(1, tiles):
        frame = frame + sd[i]
    sz[f] = frame
    for k in range(1, shards):
        push(sz.at[f], sz.at[f], sz_s.at[k - 1], sz_r.at[k - 1], t, lax.rem(f + k, shards))
    both = group_sum(frame * gain) / population
    cross, delta = both[0:1], both[1:2]

    @pl.loop(0, slots)
    def _(r):
        grad = inverse * (up[span(r), :] * gain - delta - y1[span(r), :] * cross) * is_live(r)
        kept = grad.astype(BF16)
        grad = kept.astype(F32)
        g1[r] = kept
        g0[span(r), :] = earlier(grad).astype(BF16)
        g2[span(r), :] = later(grad).astype(BF16)

    hs2[0] = g1[0]
    hs2[1] = g1[jnp.clip(live - 1, 0, slots - 1)]
    halo_start(hs2, hr2, h2_s, h2_r)

    for b in range(3):
        right = g1[...].reshape(cells, chan) if b == 1 else (g0 if b == 0 else g2)[...]
        wide[...] = jnp.dot(xcat_t[...], right, preferred_element_type=F32)
        if aligned:
            for fi, p, low, size, tap, at in pieces:
                if tap % 3 == b:
                    a = tap // 3
                    dwbuf[fi, p // 2, p % 2, low:low + size, :] = wide[
                        a * chan + at:a * chan + at + size, :
                    ].astype(BF16)
        else:
            for a in range(3):
                dwf[(3 * a + b) * chan:(3 * a + b + 1) * chan, :] = wide[a * chan:(a + 1) * chan, :]
    for fi in range(shards):
        for p in range(tiles):
            low, high = p * part, min(shard, (p + 1) * part)
            if high <= low:
                dwbuf[fi, p // 2, p % 2] = jnp.zeros((part, chan), BF16)
            elif not aligned:
                rows = dwf[fi * shard + low:fi * shard + high, :]
                if high - low < part:
                    rows = jnp.concatenate([rows, jnp.zeros((part - high + low, chan), F32)], axis=0)
                dwbuf[fi, p // 2, p % 2] = rows.astype(BF16)
            elif high - low < part:
                dwbuf[fi, p // 2, p % 2, high - low:part, :] = jnp.zeros((part - high + low, chan), BF16)

    order = list(range(1, shards)) + [0]
    for k in order:
        fd = lax.rem(f + k, shards)
        push(dwbuf.at[fd, :, 1 - c], sbuf.at[k], b_s.at[k], b_r.at[k], sibling, f)
    for k in order:
        fd = lax.rem(f + k, shards)
        copy(sbuf.at[k], sbuf.at[k], b_s.at[k], b_r.at[k], sibling, f).wait_recv()
        for j in range(1, chips):
            to = peer_chip(j)
            pbuf[k, j - 1] = (dwbuf[fd, to, c].astype(F32) + sbuf[k, to].astype(F32)).astype(BF16)
            push(pbuf.at[k, j - 1], qbuf.at[k, j - 1], q_s.at[k, j - 1], q_r.at[k, j - 1], to * 2 + c, f)

    halo_wait(hs2, hr2, h2_s, h2_r)
    grad_below = hr2[1].astype(F32)
    for j in range(slots + 2):
        if j == 0:
            flat = hr2[0]
        elif j <= slots:
            flat = (g1[j - 1].astype(F32) + grad_below * is_end(j - 1)).astype(BF16)
        else:
            flat = (grad_below * is_end(slots)).astype(BF16)
        for a in range(3):
            r = j - 2 + a
            if 0 <= r < slots:
                cat[r * cols:(r + 1) * cols, a * chan:(a + 1) * chan] = flat
    three(cat, wt, (2, 1, 0))

    @pl.loop(0, slots)
    def _(r):
        rows = y1[span(r), :] + later(y0[span(r), :]) + earlier(y2[span(r), :])
        ig_ref[r] = (rows * is_live(r)).T.astype(BF16)

    ig_out = pltpu.make_async_copy(ig_ref, ig_any, loc.at[2])
    ig_out.start()

    own = None
    for k in order:
        fd = lax.rem(f + k, shards)
        summed = dwbuf[fd, ch, c].astype(F32) + sbuf[k, ch].astype(F32)
        for j in range(1, chips):
            block = qbuf.at[k, j - 1]
            copy(block, block, q_s.at[k, j - 1], q_r.at[k, j - 1], t, f).wait_recv()
            summed = summed + qbuf[k, j - 1].astype(F32)
        if k == 0:
            own = summed
        else:
            zbuf[k - 1] = summed.astype(BF16)
            push(zbuf.at[k - 1], rbuf.at[k - 1], r_s.at[k - 1], r_r.at[k - 1], t, fd)
    for k in range(1, shards):
        block = rbuf.at[k - 1]
        copy(block, block, r_s.at[k - 1], r_r.at[k - 1], t, f).wait_recv()
        own = own + rbuf[k - 1].astype(F32)
    fbuf[t] = own.astype(BF16)
    mine = fbuf.at[t]
    for j in range(1, chips):
        push(mine, mine, f_s.at[j - 1], f_r.at[j - 1], peer_chip(j) * 2 + c, f)
    push(mine, mine, e_s.at[0], e_r.at[0], sibling, f)

    scale = float(shards * ROWS_MEAN * tiles * cols) ** (-0.5)
    for k in range(1, shards):
        block = sz.at[lax.rem(f + shards - k, shards)]
        copy(block, block, sz_s.at[k - 1], sz_r.at[k - 1], t, f).wait_recv()
    every = sz[0]
    for i in range(1, shards):
        every = every + sz[i]
    gg_ref[...] = (every[0:1] * scale).reshape(chan)
    bg_ref[...] = (every[1:2] * scale).reshape(chan)

    for j in range(1, chips):
        block = fbuf.at[from_chip(j) * 2 + c]
        copy(block, block, f_s.at[j - 1], f_r.at[j - 1], t, f).wait_recv()
        push(block, block, e_s.at[j], e_r.at[j], sibling, f)
    for j in range(chips):
        block = fbuf.at[from_chip(j) * 2 + (1 - c)]
        copy(block, block, e_s.at[j], e_r.at[j], sibling, f).wait_recv()

    for p in range(-(-shard // part)):
        low, high = p * part, min(shard, (p + 1) * part)
        wrow[low:high, :] = fbuf[p].astype(F32)[:high - low]
    wg_ref[...] = wrow[...].T.astype(BF16)

    act_out.wait()
    ig_out.wait()
    for made in sent:
        made.wait_send()


def adam(
    scale, act_ref, ig_ref, grad_ref, w_ref, m1_ref, m2_ref, gg_ref, bg_ref,
    act_out, ig_out, wg_out, nw_out, n1_out, n2_out, gg_out, bg_out,
):
    act_out[...] = act_ref[...]
    ig_out[...] = ig_ref[...]
    gg_out[...] = gg_ref[...]
    bg_out[...] = bg_ref[...]
    grad = grad_ref[...].astype(F32) * scale
    wg_out[...] = grad
    first = 0.9 * m1_ref[...] + 0.1 * grad
    second = 0.999 * m2_ref[...] + 0.001 * grad * grad
    n1_out[...] = first
    n2_out[...] = second
    first_fix = first / (1.0 - 0.9**10)
    second_fix = second / (1.0 - 0.999**10)
    nw_out[...] = w_ref[...] - 0.01 * first_fix / (jnp.sqrt(second_fix) + 1e-08)


def swapped(array):
    return jnp.swapaxes(array, 1, 2)


def local(
    images, tile_rows, cotangent, master_weight, norm_gain, norm_bias, first_moment, second_moment
):
    slots, cols, chan = images.shape[2:]
    cells = slots * cols
    shard = master_weight.shape[0]
    tiles = lax.axis_size("tile")
    shards = lax.axis_size("fsdp")
    chips = tiles // 2
    part = -(-shard // (tiles * 16)) * 16
    anywhere = pl.BlockSpec(memory_space=pl.ANY)
    vmem = pl.BlockSpec(memory_space=pltpu.VMEM)
    dma = pltpu.SemaphoreType.DMA
    aligned = shard % 16 == 0
    rows_out = jax.ShapeDtypeStruct((chan, shard), F32)
    grad_out = jax.ShapeDtypeStruct((chan, shard), BF16)
    pair = [dma((2,))] * 2
    picture = jax.ShapeDtypeStruct((slots, chan, cols), BF16)
    line = jax.ShapeDtypeStruct((chan,), F32)
    flops = 3 * 2 * cells * 9 * chan * chan
    result = pl.pallas_call(
        functools.partial(kernel, tiles, shards, part),
        out_shape=(picture, picture, grad_out, line, line),
        in_specs=[
            pl.BlockSpec(memory_space=pltpu.SMEM), vmem, anywhere, vmem, vmem, vmem
        ],
        out_specs=(anywhere, anywhere) + (vmem,) * 3,
        scratch_shapes=[
            pltpu.VMEM((slots, chan, cols), BF16),
            pltpu.VMEM((slots, chan, cols), BF16),
            pltpu.VMEM((slots, chan, cols), BF16),
            pltpu.VMEM((chan, chan), F32),
            pltpu.VMEM((shard, chan), F32),
            dma((3,)),
            pltpu.VMEM((shards, tiles, part, chan), BF16),
            pltpu.VMEM((3, 3 * chan, chan), BF16),
            pltpu.VMEM((3, 3 * chan, chan), BF16),
            pltpu.VMEM((3 * chan, chan), F32),
            pltpu.VMEM((cells, 3 * chan), BF16),
            pltpu.VMEM((3 * chan, cells), BF16),
            pltpu.VMEM((cells, 3 * chan), BF16),
            pltpu.VMEM((cells, chan), F32),
            pltpu.VMEM((cells, chan), F32),
            pltpu.VMEM((cells, chan), F32),
            pltpu.VMEM((cells, chan), F32),
            pltpu.VMEM((cells, chan), BF16),
            pltpu.VMEM((slots, cols, chan), BF16),
            pltpu.VMEM((cells, chan), BF16),
            pltpu.VMEM((2, chan, cols), BF16),
            pltpu.VMEM((2, chan, cols), BF16),
            pltpu.VMEM((2, cols, chan), BF16),
            pltpu.VMEM((2, cols, chan), BF16),
            pltpu.VMEM((tiles, 8, chan), F32),
            pltpu.VMEM((tiles, 8, chan), F32),
            pltpu.VMEM((shards, 8, chan), F32),
            pltpu.VMEM((shards, chips, 2, part, chan), BF16),
            pltpu.VMEM((8 if aligned else shards * shard, chan), F32),
            pltpu.VMEM((shards, chips, part, chan), BF16),
            pltpu.VMEM((shards, chips - 1, part, chan), BF16),
            pltpu.VMEM((shards, chips - 1, part, chan), BF16),
            pltpu.VMEM((shards - 1, part, chan), BF16),
            pltpu.VMEM((shards - 1, part, chan), BF16),
            pltpu.VMEM((tiles, part, chan), BF16),
            dma((shards - 1,)), dma((shards - 1,)),
            dma((shards - 1, chips - 1)), dma((shards - 1, chips - 1)),
            dma((shards - 1, chips)), dma((shards - 1, chips)),
            *pair, *pair,
            dma((tiles - 1,)), dma((tiles - 1,)),
            dma((tiles - 1,)), dma((tiles - 1,)),
            dma((shards - 1,)), dma((shards - 1,)),
            dma((shards,)), dma((shards,)),
            dma((shards, chips - 1)), dma((shards, chips - 1)),
            dma((shards - 1,)), dma((shards - 1,)),
            dma((chips - 1,)), dma((chips - 1,)),
            dma((chips,)), dma((chips,)),
        ],
        compiler_params=pltpu.CompilerParams(
            collective_id=0, has_side_effects=True, vmem_limit_bytes=58 * 2**20
        ),
        cost_estimate=pl.CostEstimate(
            flops=flops, bytes_accessed=16 * 2**20, transcendentals=cells * chan
        ),
        name="conv_block",
    )(
        tile_rows, swapped(images[0, 0]), swapped(cotangent[0, 0]), master_weight.T,
        norm_gain, norm_bias,
    )
    act, ig, wg, gg, bg = result
    steps = 4
    slab = pl.BlockSpec((slots // steps, chan, cols), lambda i: (i, 0, 0))
    strip = pl.BlockSpec((chan // steps, shard), lambda i: (i, 0))
    whole = pl.BlockSpec((chan,), lambda i: (0,))
    scale = float(shards * ROWS_MEAN * tiles * cols) ** (-0.5)
    act, ig, wg, nw, n1, n2, gg, bg = pl.pallas_call(
        functools.partial(adam, scale),
        grid=(steps,),
        out_shape=(picture, picture, rows_out, rows_out, rows_out, rows_out, line, line),
        in_specs=[slab, slab, strip, strip, strip, strip, whole, whole],
        out_specs=(slab, slab, strip, strip, strip, strip, whole, whole),
        compiler_params=pltpu.CompilerParams(vmem_limit_bytes=32 * 2**20),
        name="adam_step",
    )(act, ig, wg, master_weight.T, first_moment.T, second_moment.T, gg, bg)
    act, ig = swapped(act).reshape(images.shape), swapped(ig).reshape(images.shape)
    return (act, ig, wg.T, nw.T, n1.T, n2.T, gg, bg)


def solution(mesh):
    tiled = P("fsdp", "tile", None, None, None)
    rows = P("fsdp", None)
    return jax.shard_map(
        local,
        mesh=mesh,
        in_specs=(tiled, P("fsdp", "tile"), tiled, rows, P(), P(), rows, rows),
        out_specs=(tiled, tiled, rows, rows, rows, rows, P(), P()),
        check_vma=False,
    )
```

```python
import functools

import jax
import jax.numpy as jnp
from jax import lax
from jax.experimental import pallas as pl
from jax.experimental.pallas import tpu as pltpu
from jax.sharding import PartitionSpec as P

GROUPS = 32
ROWS_MEAN = 5
MESH = pl.DeviceIdType.MESH
F32 = jnp.float32
BF16 = jnp.bfloat16


def row_pieces(total, shards, shard, part, block):
    found = []
    for f in range(shards):
        for p in range(-(-shard // part)):
            low, high = f * shard + p * part, f * shard + min(shard, (p + 1) * part)
            at = low
            while at < high:
                end = min(high, (at // block + 1) * block)
                found.append((f, p, at - low, end - at, at // block, at % block))
                at = end
    return found


def kernel(
    tiles, shards, part,
    rows_ref, x_ref, ct_any, w_ref, gain_ref, bias_ref,
    act_any, ig_any, wg_ref, gg_ref, bg_ref,
    ct_ref, act_ref, ig_ref, same_ref, wrow, loc,
    gath, wb, wt, wide, xcat, xcat_t, cat, y0, y1, y2, up, g0, g1, g2,
    hs, hr, hs2, hr2, st, sd, sz,
    dwbuf, dwf, sbuf, pbuf, qbuf, zbuf, rbuf, fbuf,
    z_s, z_r, p_s, p_r, s_s, s_r, h_s, h_r, h2_s, h2_r, st_s, st_r, sd_s, sd_r, sz_s, sz_r,
    b_s, b_r, q_s, q_r, r_s, r_r, f_s, f_r, e_s, e_r,
):
    slots, chan, cols = x_ref.shape
    cells = slots * cols
    shard = w_ref.shape[1]
    total = shards * shard
    chips = tiles // 2
    t = lax.axis_index("tile")
    f = lax.axis_index("fsdp")
    ch, c = t // 2, t % 2
    sibling = ch * 2 + (1 - c)
    live = rows_ref[0, 0]
    aligned = shard % 16 == 0
    sent = []

    def peer_chip(j):
        return lax.rem(ch + j, chips)

    def from_chip(j):
        return lax.rem(ch + chips - j, chips)

    def copy(src, dst, send, recv, to_tile, to_shard):
        return pltpu.make_async_remote_copy(
            src_ref=src, dst_ref=dst, send_sem=send, recv_sem=recv,
            device_id=(to_tile, to_shard), device_id_type=MESH,
        )

    def push(*args):
        made = copy(*args)
        made.start()
        sent.append(made)

    barrier = pltpu.get_barrier_semaphore()
    for j in range(1, tiles):
        pl.semaphore_signal(barrier, inc=1, device_id=(lax.rem(t + j, tiles), f), device_id_type=MESH)
    for k in range(1, shards):
        pl.semaphore_signal(barrier, inc=1, device_id=(t, lax.rem(f + k, shards)), device_id_type=MESH)

    ct_in = pltpu.make_async_copy(ct_any, ct_ref, loc.at[0])
    ct_in.start()

    wrow[...] = w_ref[...].T
    for p in range(tiles):
        low, high = p * part, min(shard, (p + 1) * part)
        if high <= low:
            gath[f, p] = jnp.zeros((part, chan), BF16)
        else:
            rows = wrow[low:high, :]
            if high - low < part:
                rows = jnp.concatenate([rows, jnp.zeros((part - high + low, chan), F32)], axis=0)
            gath[f, p] = rows.astype(BF16)
    hs[0] = x_ref[0]
    hs[1] = x_ref[jnp.clip(live - 1, 0, slots - 1)]
    pl.semaphore_wait(barrier, tiles + shards - 2)

    for k in range(1, shards):
        push(gath.at[f, t], gath.at[f, t], z_s.at[k - 1], z_r.at[k - 1], t, lax.rem(f + k, shards))

    def halo_copies(src, dst, send, recv):
        up_copy = copy(src.at[0], dst.at[1], send.at[0], recv.at[1], lax.rem(t + tiles - 1, tiles), f)
        down_copy = copy(src.at[1], dst.at[0], send.at[1], recv.at[0], lax.rem(t + 1, tiles), f)
        return up_copy, down_copy

    def halo_start(src, dst, send, recv):
        up_copy, down_copy = halo_copies(src, dst, send, recv)

        @pl.when(t > 0)
        def _():
            up_copy.start()

        @pl.when(t == 0)
        def _():
            dst[0] = jnp.zeros(dst.shape[1:], BF16)

        @pl.when(t < tiles - 1)
        def _():
            down_copy.start()

        @pl.when(t == tiles - 1)
        def _():
            dst[1] = jnp.zeros(dst.shape[1:], BF16)

    def halo_wait(src, dst, send, recv):
        up_copy, down_copy = halo_copies(src, dst, send, recv)

        @pl.when(t > 0)
        def _():
            up_copy.wait_send()
            down_copy.wait_recv()

        @pl.when(t < tiles - 1)
        def _():
            down_copy.wait_send()
            up_copy.wait_recv()

    halo_start(hs, hr, h_s, h_r)

    for k in range(1, shards):
        fs = lax.rem(f + shards - k, shards)
        block = gath.at[fs, t]
        copy(block, block, z_s.at[k - 1], z_r.at[k - 1], t, f).wait_recv()
        for j in range(1, chips):
            push(block, block, p_s.at[k - 1, j - 1], p_r.at[k - 1, j - 1], peer_chip(j) * 2 + c, f)
        push(block, block, s_s.at[k - 1, 0], s_r.at[k - 1, 0], sibling, f)

    halo_wait(hs, hr, h_s, h_r)
    below = hr[1].astype(F32)

    def is_live(r):
        return (r < live).astype(F32)

    def is_end(r):
        return (r == live).astype(F32)

    for j in range(slots + 2):
        if j == 0:
            value = hr[0].astype(F32)
        elif j <= slots:
            value = x_ref[j - 1].astype(F32) * is_live(j - 1) + below * is_end(j - 1)
        else:
            value = below * is_end(slots)
        flat, turned = value.T.astype(BF16), value.astype(BF16)
        for a in range(3):
            r = j - a
            if 0 <= r < slots:
                xcat[r * cols:(r + 1) * cols, a * chan:(a + 1) * chan] = flat
                xcat_t[a * chan:(a + 1) * chan, r * cols:(r + 1) * cols] = turned

    ct_in.wait()
    for r in range(slots):
        up[r * cols:(r + 1) * cols, :] = ct_ref[r].astype(F32).T
    across = lax.broadcasted_iota(jnp.int32, (chan, chan), 1).astype(F32)
    down = lax.broadcasted_iota(jnp.int32, (chan, chan), 0).astype(F32)
    per = float(chan // GROUPS)
    same_ref[...] = (jnp.floor((across + 0.5) / per) == jnp.floor((down + 0.5) / per)).astype(F32)

    for k in range(1, shards):
        fs = lax.rem(f + shards - k, shards)
        for j in range(1, chips):
            block = gath.at[fs, from_chip(j) * 2 + c]
            copy(block, block, p_s.at[k - 1, j - 1], p_r.at[k - 1, j - 1], t, f).wait_recv()
            push(block, block, s_s.at[k - 1, j], s_r.at[k - 1, j], sibling, f)
    for k in range(1, shards):
        fs = lax.rem(f + shards - k, shards)
        for j in range(chips):
            block = gath.at[fs, from_chip(j) * 2 + (1 - c)]
            copy(block, block, s_s.at[k - 1, j], s_r.at[k - 1, j], sibling, f).wait_recv()

    pieces = row_pieces(total, shards, shard, part, chan)
    if aligned:
        for fi, p, low, size, tap, at in pieces:
            a, b = tap // 3, tap % 3
            wb[b, a * chan + at:a * chan + at + size, :] = gath[fi, p, low:low + size, :]
    else:
        for fi in range(shards):
            for p in range(-(-shard // part)):
                size = min(shard - p * part, part)
                dwf[fi * shard + p * part:fi * shard + p * part + size, :] = (
                    gath[fi, p].astype(F32)[:size]
                )
        for tap in range(9):
            a, b = tap // 3, tap % 3
            wb[b, a * chan:(a + 1) * chan, :] = dwf[tap * chan:(tap + 1) * chan, :].astype(BF16)

    half = cells // 2

    def three(source, weights, order):
        @pl.loop(0, 2)
        def _(h):
            at = pl.ds(pl.multiple_of(h * half, half), half)
            left = source[at, :]
            for b, into in zip(order, (y0, y1, y2)):
                into[at, :] = jnp.dot(left, weights[b], preferred_element_type=F32)

    column = lax.broadcasted_iota(jnp.int32, (cols, chan), 0)

    def later(rows):
        return jnp.where(column == 0, 0.0, pltpu.roll(rows, 1, 0))

    def earlier(rows):
        return jnp.where(column == cols - 1, 0.0, pltpu.roll(rows, cols - 1, 0))

    def span(r):
        return pl.ds(pl.multiple_of(r * cols, cols), cols)

    def group_sum(row):
        return jnp.dot(row, same_ref[...], precision=lax.Precision.HIGHEST, preferred_element_type=F32)

    three(xcat, wb, (0, 1, 2))

    def mix(r, sums):
        rows = y1[span(r), :] + later(y0[span(r), :]) + earlier(y2[span(r), :])
        y1[span(r), :] = rows
        return sums + jnp.sum(rows, axis=0, keepdims=True) * is_live(r)

    zero_row = jnp.zeros((1, chan), F32)
    own_count = live.astype(F32) * (cols * (chan // GROUPS))
    count_row = jnp.zeros((1, chan), F32) + own_count
    own_mean = group_sum(lax.fori_loop(0, slots, mix, zero_row)) / count_row

    def squares(r, sums):
        off = y1[span(r), :] - own_mean
        return sums + jnp.sum(off * off, axis=0, keepdims=True) * is_live(r)

    own_square = group_sum(lax.fori_loop(0, slots, squares, zero_row))

    def tile_share(buffer, send, recv):
        for j in range(1, tiles):
            push(buffer.at[t], buffer.at[t], send.at[j - 1], recv.at[j - 1], lax.rem(t + j, tiles), f)

    def tile_wait(buffer, send, recv):
        for j in range(1, tiles):
            block = buffer.at[lax.rem(t + tiles - j, tiles)]
            copy(block, block, send.at[j - 1], recv.at[j - 1], t, f).wait_recv()

    st[t] = jnp.concatenate(
        [own_mean, own_square, count_row, jnp.zeros((5, chan), F32)], axis=0
    )
    tile_share(st, st_s, st_r)

    for tap in range(9):
        a, b = tap // 3, tap % 3
        block = wb[b, a * chan:(a + 1) * chan, :].astype(F32)
        wt[b, a * chan:(a + 1) * chan, :] = block.T.astype(BF16)

    tile_wait(st, st_s, st_r)
    population = float(ROWS_MEAN * tiles * cols * (chan // GROUPS))
    mean = zero_row
    for i in range(tiles):
        mean = mean + st[i, 0:1, :] * st[i, 2:3, :]
    mean = mean / population
    spread = zero_row
    for i in range(tiles):
        apart = st[i, 0:1, :] - mean
        spread = spread + st[i, 1:2, :] + st[i, 2:3, :] * apart * apart
    inverse = lax.rsqrt(spread / population + 1e-05)
    gain, bias = gain_ref[...].reshape(1, chan), bias_ref[...].reshape(1, chan)

    def gate(r, sums):
        gains, biases = sums
        mask = is_live(r)
        normed = (y1[span(r), :] - mean) * inverse
        shifted = normed * gain + bias
        s = jax.nn.sigmoid(shifted)
        act_ref[r] = (shifted * s * mask).T.astype(BF16)
        dshift = up[span(r), :] * mask * s * (1.0 + shifted * (1.0 - s))
        y1[span(r), :] = normed
        up[span(r), :] = dshift
        return (
            gains + jnp.sum(dshift * normed, axis=0, keepdims=True),
            biases + jnp.sum(dshift, axis=0, keepdims=True),
        )

    own_gain, own_bias = lax.fori_loop(0, slots, gate, (zero_row, zero_row))
    act_out = pltpu.make_async_copy(act_ref, act_any, loc.at[1])
    act_out.start()
    sd[t] = jnp.concatenate([own_gain, own_bias, jnp.zeros((6, chan), F32)], axis=0)
    tile_share(sd, sd_s, sd_r)
    tile_wait(sd, sd_s, sd_r)
    frame = sd[0]
    for i in range(1, tiles):
        frame = frame + sd[i]
    sz[f] = frame
    for k in range(1, shards):
        push(sz.at[f], sz.at[f], sz_s.at[k - 1], sz_r.at[k - 1], t, lax.rem(f + k, shards))
    both = group_sum(frame * gain) / population
    cross, delta = both[0:1], both[1:2]

    @pl.loop(0, slots)
    def _(r):
        grad = inverse * (up[span(r), :] * gain - delta - y1[span(r), :] * cross) * is_live(r)
        kept = grad.astype(BF16)
        grad = kept.astype(F32)
        g1[r] = kept
        g0[span(r), :] = earlier(grad).astype(BF16)
        g2[span(r), :] = later(grad).astype(BF16)

    hs2[0] = g1[0]
    hs2[1] = g1[jnp.clip(live - 1, 0, slots - 1)]
    halo_start(hs2, hr2, h2_s, h2_r)

    def sibling_copy(fi):
        return copy(
            dwbuf.at[fi, :, 1 - c], sbuf.at[fi], b_s.at[fi], b_r.at[fi], sibling, f
        )

    def finish_shard(fi):
        for p in range(tiles):
            low, high = p * part, min(shard, (p + 1) * part)
            if high <= low:
                dwbuf[fi, p // 2, p % 2] = jnp.zeros((part, chan), BF16)
            elif not aligned:
                rows = dwf[fi * shard + low:fi * shard + high, :]
                if high - low < part:
                    rows = jnp.concatenate([rows, jnp.zeros((part - high + low, chan), F32)], axis=0)
                dwbuf[fi, p // 2, p % 2] = rows.astype(BF16)
            elif high - low < part:
                dwbuf[fi, p // 2, p % 2, high - low:part, :] = jnp.zeros((part - high + low, chan), BF16)
        made = sibling_copy(fi)
        made.start()
        sent.append(made)

    def plane_send(fi):
        sibling_copy(fi).wait_recv()
        for j in range(1, chips):
            to = peer_chip(j)
            pbuf[fi, j - 1] = (dwbuf[fi, to, c].astype(F32) + sbuf[fi, to].astype(F32)).astype(BF16)
            push(pbuf.at[fi, j - 1], qbuf.at[fi, j - 1], q_s.at[fi, j - 1], q_r.at[fi, j - 1], to * 2 + c, f)

    done, passed = 0, 0
    for a in range(3):
        left = xcat_t[a * chan:(a + 1) * chan, :]
        for b in range(3):
            right = g1[...].reshape(cells, chan) if b == 1 else (g0 if b == 0 else g2)[...]
            block = jnp.dot(left, right, preferred_element_type=F32)
            if aligned:
                wide[...] = block
                for fi, p, low, size, tap, at in pieces:
                    if tap == 3 * a + b:
                        dwbuf[fi, p // 2, p % 2, low:low + size, :] = wide[at:at + size, :].astype(BF16)
            else:
                dwf[(3 * a + b) * chan:(3 * a + b + 1) * chan, :] = block
        ready = done
        while done < shards and (done + 1) * shard <= 3 * (a + 1) * chan:
            finish_shard(done)
            done += 1
        while passed < ready:
            plane_send(passed)
            passed += 1
    while passed < shards:
        plane_send(passed)
        passed += 1

    halo_wait(hs2, hr2, h2_s, h2_r)
    grad_below = hr2[1].astype(F32)
    for j in range(slots + 2):
        if j == 0:
            flat = hr2[0]
        elif j <= slots:
            flat = (g1[j - 1].astype(F32) + grad_below * is_end(j - 1)).astype(BF16)
        else:
            flat = (grad_below * is_end(slots)).astype(BF16)
        for a in range(3):
            r = j - 2 + a
            if 0 <= r < slots:
                cat[r * cols:(r + 1) * cols, a * chan:(a + 1) * chan] = flat
    three(cat, wt, (2, 1, 0))

    @pl.loop(0, slots)
    def _(r):
        rows = y1[span(r), :] + later(y0[span(r), :]) + earlier(y2[span(r), :])
        ig_ref[r] = (rows * is_live(r)).T.astype(BF16)

    ig_out = pltpu.make_async_copy(ig_ref, ig_any, loc.at[2])
    ig_out.start()

    def shard_copy(fi):
        return copy(zbuf.at[fi], rbuf.at[f], r_s.at[fi], r_r.at[f], t, fi)

    for fi in range(shards):
        summed = dwbuf[fi, ch, c].astype(F32) + sbuf[fi, ch].astype(F32)
        for j in range(1, chips):
            block = qbuf.at[fi, j - 1]
            copy(block, block, q_s.at[fi, j - 1], q_r.at[fi, j - 1], t, f).wait_recv()
            summed = summed + qbuf[fi, j - 1].astype(F32)
        zbuf[fi] = summed.astype(BF16)

        @pl.when(f != fi)
        def _():
            shard_copy(fi).start()

    own = zbuf[f].astype(F32)
    for k in range(1, shards):
        fs = lax.rem(f + k, shards)
        block = rbuf.at[fs]
        copy(block, block, r_s.at[fs], r_r.at[fs], t, f).wait_recv()
        own = own + rbuf[fs].astype(F32)
    fbuf[t] = own.astype(BF16)
    mine = fbuf.at[t]
    for j in range(1, chips):
        push(mine, mine, f_s.at[j - 1], f_r.at[j - 1], peer_chip(j) * 2 + c, f)
    push(mine, mine, e_s.at[0], e_r.at[0], sibling, f)

    scale = float(shards * ROWS_MEAN * tiles * cols) ** (-0.5)
    for k in range(1, shards):
        block = sz.at[lax.rem(f + shards - k, shards)]
        copy(block, block, sz_s.at[k - 1], sz_r.at[k - 1], t, f).wait_recv()
    every = sz[0]
    for i in range(1, shards):
        every = every + sz[i]
    gg_ref[...] = (every[0:1] * scale).reshape(chan)
    bg_ref[...] = (every[1:2] * scale).reshape(chan)

    for j in range(1, chips):
        block = fbuf.at[from_chip(j) * 2 + c]
        copy(block, block, f_s.at[j - 1], f_r.at[j - 1], t, f).wait_recv()
        push(block, block, e_s.at[j], e_r.at[j], sibling, f)
    for j in range(chips):
        block = fbuf.at[from_chip(j) * 2 + (1 - c)]
        copy(block, block, e_s.at[j], e_r.at[j], sibling, f).wait_recv()

    for p in range(-(-shard // part)):
        low, high = p * part, min(shard, (p + 1) * part)
        wrow[low:high, :] = fbuf[p].astype(F32)[:high - low]
    wg_ref[...] = wrow[...].T.astype(BF16)

    for fi in range(shards):

        @pl.when(f != fi)
        def _():
            shard_copy(fi).wait_send()

    act_out.wait()
    ig_out.wait()
    for made in sent:
        made.wait_send()


def adam(
    scale, act_ref, ig_ref, grad_ref, w_ref, m1_ref, m2_ref, gg_ref, bg_ref,
    act_out, ig_out, wg_out, nw_out, n1_out, n2_out, gg_out, bg_out,
):
    act_out[...] = act_ref[...]
    ig_out[...] = ig_ref[...]
    gg_out[...] = gg_ref[...]
    bg_out[...] = bg_ref[...]
    grad = grad_ref[...].astype(F32) * scale
    wg_out[...] = grad
    first = 0.9 * m1_ref[...] + 0.1 * grad
    second = 0.999 * m2_ref[...] + 0.001 * grad * grad
    n1_out[...] = first
    n2_out[...] = second
    first_fix = first / (1.0 - 0.9**10)
    second_fix = second / (1.0 - 0.999**10)
    nw_out[...] = w_ref[...] - 0.01 * first_fix / (jnp.sqrt(second_fix) + 1e-08)


def swapped(array):
    return jnp.swapaxes(array, 1, 2)


def local(
    images, tile_rows, cotangent, master_weight, norm_gain, norm_bias, first_moment, second_moment
):
    slots, cols, chan = images.shape[2:]
    cells = slots * cols
    shard = master_weight.shape[0]
    tiles = lax.axis_size("tile")
    shards = lax.axis_size("fsdp")
    chips = tiles // 2
    part = -(-shard // (tiles * 16)) * 16
    anywhere = pl.BlockSpec(memory_space=pl.ANY)
    vmem = pl.BlockSpec(memory_space=pltpu.VMEM)
    dma = pltpu.SemaphoreType.DMA
    aligned = shard % 16 == 0
    rows_out = jax.ShapeDtypeStruct((chan, shard), F32)
    grad_out = jax.ShapeDtypeStruct((chan, shard), BF16)
    pair = [dma((2,))] * 2
    picture = jax.ShapeDtypeStruct((slots, chan, cols), BF16)
    line = jax.ShapeDtypeStruct((chan,), F32)
    flops = 3 * 2 * cells * 9 * chan * chan
    result = pl.pallas_call(
        functools.partial(kernel, tiles, shards, part),
        out_shape=(picture, picture, grad_out, line, line),
        in_specs=[
            pl.BlockSpec(memory_space=pltpu.SMEM), vmem, anywhere, vmem, vmem, vmem
        ],
        out_specs=(anywhere, anywhere) + (vmem,) * 3,
        scratch_shapes=[
            pltpu.VMEM((slots, chan, cols), BF16),
            pltpu.VMEM((slots, chan, cols), BF16),
            pltpu.VMEM((slots, chan, cols), BF16),
            pltpu.VMEM((chan, chan), F32),
            pltpu.VMEM((shard, chan), F32),
            dma((3,)),
            pltpu.VMEM((shards, tiles, part, chan), BF16),
            pltpu.VMEM((3, 3 * chan, chan), BF16),
            pltpu.VMEM((3, 3 * chan, chan), BF16),
            pltpu.VMEM((chan, chan), F32),
            pltpu.VMEM((cells, 3 * chan), BF16),
            pltpu.VMEM((3 * chan, cells), BF16),
            pltpu.VMEM((cells, 3 * chan), BF16),
            pltpu.VMEM((cells, chan), F32),
            pltpu.VMEM((cells, chan), F32),
            pltpu.VMEM((cells, chan), F32),
            pltpu.VMEM((cells, chan), F32),
            pltpu.VMEM((cells, chan), BF16),
            pltpu.VMEM((slots, cols, chan), BF16),
            pltpu.VMEM((cells, chan), BF16),
            pltpu.VMEM((2, chan, cols), BF16),
            pltpu.VMEM((2, chan, cols), BF16),
            pltpu.VMEM((2, cols, chan), BF16),
            pltpu.VMEM((2, cols, chan), BF16),
            pltpu.VMEM((tiles, 8, chan), F32),
            pltpu.VMEM((tiles, 8, chan), F32),
            pltpu.VMEM((shards, 8, chan), F32),
            pltpu.VMEM((shards, chips, 2, part, chan), BF16),
            pltpu.VMEM((8 if aligned else shards * shard, chan), F32),
            pltpu.VMEM((shards, chips, part, chan), BF16),
            pltpu.VMEM((shards, chips - 1, part, chan), BF16),
            pltpu.VMEM((shards, chips - 1, part, chan), BF16),
            pltpu.VMEM((shards, part, chan), BF16),
            pltpu.VMEM((shards, part, chan), BF16),
            pltpu.VMEM((tiles, part, chan), BF16),
            dma((shards - 1,)), dma((shards - 1,)),
            dma((shards - 1, chips - 1)), dma((shards - 1, chips - 1)),
            dma((shards - 1, chips)), dma((shards - 1, chips)),
            *pair, *pair,
            dma((tiles - 1,)), dma((tiles - 1,)),
            dma((tiles - 1,)), dma((tiles - 1,)),
            dma((shards - 1,)), dma((shards - 1,)),
            dma((shards,)), dma((shards,)),
            dma((shards, chips - 1)), dma((shards, chips - 1)),
            dma((shards,)), dma((shards,)),
            dma((chips - 1,)), dma((chips - 1,)),
            dma((chips,)), dma((chips,)),
        ],
        compiler_params=pltpu.CompilerParams(
            collective_id=0, has_side_effects=True, vmem_limit_bytes=58 * 2**20
        ),
        cost_estimate=pl.CostEstimate(
            flops=flops, bytes_accessed=16 * 2**20, transcendentals=cells * chan
        ),
        name="conv_block",
    )(
        tile_rows, swapped(images[0, 0]), swapped(cotangent[0, 0]), master_weight.T,
        norm_gain, norm_bias,
    )
    act, ig, wg, gg, bg = result
    steps = 4
    slab = pl.BlockSpec((slots // steps, chan, cols), lambda i: (i, 0, 0))
    strip = pl.BlockSpec((chan // steps, shard), lambda i: (i, 0))
    whole = pl.BlockSpec((chan,), lambda i: (0,))
    scale = float(shards * ROWS_MEAN * tiles * cols) ** (-0.5)
    act, ig, wg, nw, n1, n2, gg, bg = pl.pallas_call(
        functools.partial(adam, scale),
        grid=(steps,),
        out_shape=(picture, picture, rows_out, rows_out, rows_out, rows_out, line, line),
        in_specs=[slab, slab, strip, strip, strip, strip, whole, whole],
        out_specs=(slab, slab, strip, strip, strip, strip, whole, whole),
        compiler_params=pltpu.CompilerParams(vmem_limit_bytes=58 * 2**20),
        name="adam_step",
    )(act, ig, wg, master_weight.T, first_moment.T, second_moment.T, gg, bg)
    act, ig = swapped(act).reshape(images.shape), swapped(ig).reshape(images.shape)
    return (act, ig, wg.T, nw.T, n1.T, n2.T, gg, bg)


def solution(mesh):
    tiled = P("fsdp", "tile", None, None, None)
    rows = P("fsdp", None)
    return jax.shard_map(
        local,
        mesh=mesh,
        in_specs=(tiled, P("fsdp", "tile"), tiled, rows, P(), P(), rows, rows),
        out_specs=(tiled, tiled, rows, rows, rows, rows, P(), P()),
        check_vma=False,
    )
```
